32 devices in a mesh: gx: 4 (over z), gy: 8 (over y, x, core).
Axes of the slice: x: 2, y: 2, z: 4, core: 2. Of those that a mesh axis runs over, the one named last changes fastest.
Arguments:
- image_small: bfloat16 [128, 10, 10, 1024], P(('gx', 'gy')), may hold values from -21 to 21
- image_medium: bfloat16 [128, 14, 14, 1024], P(('gx', 'gy')), may hold values from -21 to 21
- image_large: bfloat16 [64, 18, 18, 1024], P(('gx', 'gy')), may hold values from -21 to 21
- cot_small: bfloat16 [128, 5, 5, 2048], P(('gx', 'gy')), may hold values from -21 to 21
- cot_medium: bfloat16 [128, 7, 7, 2048], P(('gx', 'gy')), may hold values from -21 to 21
- cot_large: bfloat16 [64, 9, 9, 2048], P(('gx', 'gy')), may hold values from -21 to 21
- counts: int32 [32, 3], P(('gx', 'gy')), may hold values from 1 to 4, as said below
- weights_a: float32 [6029312], P(('gx', 'gy')), may hold values from -1 to 1
- weights_b: float32 [4456448], P(('gx', 'gy')), may hold values from -1 to 1
- moment_a: float32 [6029312], P(('gx', 'gy')), may hold values from -0.0078125 to 0.0078125
- moment_b: float32 [4456448], P(('gx', 'gy')), may hold values from -0.0078125 to 0.0078125
- gains_narrow: float32 [4, 2, 512], replicated, may hold values from -1.5 to 1.5
- gains_wide: float32 [3, 2, 2048], replicated, may hold values from -1.5 to 1.5
- gain_moment_narrow: float32 [4, 2, 512], replicated, may hold values from -0.15625 to 0.15625
- gain_moment_wide: float32 [3, 2, 2048], replicated, may hold values from -0.15625 to 0.15625
Outputs:
- grad_small: bfloat16 [128, 10, 10, 1024], P(('gx', 'gy'))
- grad_medium: bfloat16 [128, 14, 14, 1024], P(('gx', 'gy'))
- grad_large: bfloat16 [64, 18, 18, 1024], P(('gx', 'gy'))
- new_moment_a: float32 [6029312], P(('gx', 'gy'))
- new_moment_b: float32 [4456448], P(('gx', 'gy'))
- new_gain_moment_narrow: float32 [4, 2, 512], replicated
- new_gain_moment_wide: float32 [3, 2, 2048], replicated
- layer_norms: float32 [7, 2], replicated
The draws below stay inside these ranges and needn't reach their ends.
Inputs may be any that keep to these rules, and one draw needn't show every extreme that they name: Column 0 counts present 160-pixel images of a device (at most 4), column 1 224-pixel ones (at most 4), column 2 288-pixel ones (at most 2); every device has at least one of each, and for each column some device is full.
All inputs are finite; a program needn't handle non-finite values.
Results may differ from the reference program's by a relative error of at most 0.035.
Values may be sent and summed in bfloat16 or wider, within the bound.
A program may use at most 320 MiB of HBM per device.

```python
from functools import partial
import jax
import jax.numpy as jnp
from jax import lax

C_IN = 1024
MID = 512
C_OUT = 2048
O_S = 5
O_M = 7
O_L = 9
CAP_S = 4
CAP_M = 4
CAP_L = 2
IMG_S = 128
IMG_M = 128
IMG_L = 64
ELEMS_A = 6029312
ELEMS_B = 4456448
N_GX = 4
N_GY = 8


def image_field(key, shape, spread):
    noise_key, offset_key = jax.random.split(key)
    normal_part = jnp.clip(jax.random.normal(noise_key, shape, jnp.float32), -5.0, 5.0)
    noise = normal_part
    offset = jnp.clip(spread * jax.random.normal(offset_key, (shape[0], shape[3]), jnp.float32), -2.0, 2.0)
    rising = 3.0 ** (jnp.arange(shape[0], dtype=jnp.float32) / max(shape[0] - 1, 1))
    return (noise + offset[:, None, None, :]) * rising[:, None, None, None]


def flat_weights(key, segments):
    result = []
    for ordinal, segment in enumerate(segments):
        length, fan_in = segment
        noise_key = jax.random.fold_in(key, ordinal)
        normal_part = jnp.clip(jax.random.normal(noise_key, (length,), jnp.float32), -4.0, 4.0)
        result.append(normal_part * fan_in ** (-0.5))
    return jnp.concatenate(result)


def gain_table(key, rows, width, gain_low, gain_high, offset_spread):
    gain_key, offset_key = jax.random.split(key)
    gains = jax.random.uniform(gain_key, (rows, width), jnp.float32, gain_low, gain_high)
    offsets = jnp.clip(offset_spread * jax.random.normal(offset_key, (rows, width), jnp.float32), -1.0, 1.0)
    return jnp.stack([gains, offsets], axis=1)


def draw_image_small(key, part):
    key = jax.random.fold_in(key, 11)
    shape = (IMG_S, 2 * O_S, 2 * O_S, C_IN)
    return image_field(key, shape, 0.5).astype(jnp.bfloat16)


def draw_image_medium(key, part):
    key = jax.random.fold_in(key, 12)
    shape = (IMG_M, 2 * O_M, 2 * O_M, C_IN)
    return image_field(key, shape, 0.5).astype(jnp.bfloat16)


def draw_image_large(key, part):
    key = jax.random.fold_in(key, 13)
    shape = (IMG_L, 2 * O_L, 2 * O_L, C_IN)
    return image_field(key, shape, 0.5).astype(jnp.bfloat16)


def draw_cot_small(key, part):
    key = jax.random.fold_in(key, 14)
    shape = (IMG_S, O_S, O_S, C_OUT)
    return image_field(key, shape, 0.3).astype(jnp.bfloat16)


def draw_cot_medium(key, part):
    key = jax.random.fold_in(key, 15)
    shape = (IMG_M, O_M, O_M, C_OUT)
    return image_field(key, shape, 0.3).astype(jnp.bfloat16)


def draw_cot_large(key, part):
    key = jax.random.fold_in(key, 16)
    shape = (IMG_L, O_L, O_L, C_OUT)
    return image_field(key, shape, 0.3).astype(jnp.bfloat16)


def draw_counts(key, part):
    key = jax.random.fold_in(key, 17)
    value_key, full_key = jax.random.split(key)
    devices_all = N_GX * N_GY
    capacity = jnp.array([CAP_S, CAP_M, CAP_L], jnp.int32)
    drawn = jax.random.randint(value_key, (devices_all, 3), 1, capacity[None, :] + 1)
    full_rows = jax.random.randint(full_key, (3,), 0, devices_all)
    device_ids = jnp.arange(devices_all, dtype=jnp.int32)[:, None]
    return jnp.where(device_ids == full_rows[None, :], capacity[None, :], drawn).astype(jnp.int32)


def draw_weights_a(key, part):
    key = jax.random.fold_in(key, 21)
    segments = [(C_IN * MID, C_IN), (9 * MID * MID, 9 * MID), (MID * C_OUT, MID), (C_IN * C_OUT, C_IN)]
    return flat_weights(key, segments)


def draw_weights_b(key, part):
    key = jax.random.fold_in(key, 22)
    segments = [(C_OUT * MID, C_OUT), (9 * MID * MID, 9 * MID), (MID * C_OUT, MID)]
    return flat_weights(key, segments)


def draw_gains_narrow(key, part):
    key = jax.random.fold_in(key, 23)
    return gain_table(key, 4, MID, 0.6, 1.4, 0.3)


def draw_gains_wide(key, part):
    key = jax.random.fold_in(key, 24)
    return gain_table(key, 3, C_OUT, 0.6, 1.4, 0.3)


def block_levels(stream_key, extent, cuts, least, high):
    factor_of, own = 1.0, jax.random.fold_in(stream_key, 6)
    for dim, shards_of in cuts:
        steps = jnp.exp(jax.random.uniform(jax.random.fold_in(own, dim), (shards_of,), jnp.float32, least / len(cuts), high / len(cuts)))
        factor_of = factor_of * jnp.repeat(steps, extent[dim] // shards_of).reshape([-1 if axis == dim else 1 for axis in range(len(extent))])
    return factor_of


def scatter_about(rng, dims, scale, limit, cuts=(), kind=jnp.bfloat16):
    values = scale * jax.random.normal(rng, dims, jnp.float32)
    if cuts:
        values = values * block_levels(rng, dims, cuts, -0.22, 0.18)
    return jnp.clip(values, -limit, limit).astype(kind)


def setup_inputs(seed: int = 0) -> dict:
    splits = jax.random.split(jax.random.key(seed), 16)
    image_small = draw_image_small(jax.random.fold_in(splits[15], 71), 0)
    image_medium = draw_image_medium(jax.random.fold_in(splits[15], 71), 0)
    image_large = draw_image_large(jax.random.fold_in(splits[15], 71), 0)
    cot_small = draw_cot_small(jax.random.fold_in(splits[15], 71), 0)
    cot_medium = draw_cot_medium(jax.random.fold_in(splits[15], 71), 0)
    cot_large = draw_cot_large(jax.random.fold_in(splits[15], 71), 0)
    counts = draw_counts(jax.random.fold_in(splits[15], 71), 0)
    weights_a = draw_weights_a(jax.random.fold_in(splits[15], 71), 0)
    weights_b = draw_weights_b(jax.random.fold_in(splits[15], 71), 0)
    moment_a = scatter_about(splits[9], (ELEMS_A,), 0.0005, 0.0078125, ((0, 32),), jnp.float32)
    moment_b = scatter_about(splits[10], (ELEMS_B,), 0.0005, 0.0078125, ((0, 32),), jnp.float32)
    gains_narrow = draw_gains_narrow(jax.random.fold_in(splits[15], 71), 0)
    gains_wide = draw_gains_wide(jax.random.fold_in(splits[15], 71), 0)
    gain_moment_narrow = scatter_about(splits[13], (4, 2, MID), 0.01, 0.15625, (), jnp.float32)
    gain_moment_wide = scatter_about(splits[14], (3, 2, C_OUT), 0.01, 0.15625, (), jnp.float32)
    return dict(image_small=image_small, image_medium=image_medium, image_large=image_large, cot_small=cot_small, cot_medium=cot_medium, cot_large=cot_large, counts=counts, weights_a=weights_a, weights_b=weights_b, moment_a=moment_a, moment_b=moment_b, gains_narrow=gains_narrow, gains_wide=gains_wide, gain_moment_narrow=gain_moment_narrow, gain_moment_wide=gain_moment_wide)


@jax.custom_vjp
def low(v):
    return lax.optimization_barrier(v.astype(jnp.bfloat16)).astype(jnp.float32)

@jax.custom_vjp
def low_back(v):
    return v

def low_keep(v):
    return (low(v), None)

def low_pass(kept, grad):
    return (grad,)

def back_keep(v):
    return (v, None)

def back_low(kept, grad):
    return (low(grad),)
low.defvjp(low_keep, low_pass)
low_back.defvjp(back_keep, back_low)
EPSILON = 1e-05
MOMENTUM = 0.9
LEARN_RATE = 20.0
TRUST_SCALE = 0.001
WEIGHT_DECAY = 5e-05
GAIN_RATE = 0.2

def bounds_a():
    one_end = C_IN * MID
    two_end = one_end + 9 * MID * MID
    three_end = two_end + MID * C_OUT
    return [0, one_end, two_end, three_end, three_end + C_IN * C_OUT]

def bounds_b():
    one_end = C_OUT * MID
    two_end = one_end + 9 * MID * MID
    return [0, one_end, two_end, two_end + MID * C_OUT]

def shapes_a():
    return [(C_IN, MID), (3, 3, MID, MID), (MID, C_OUT), (C_IN, C_OUT)]

def shapes_b():
    return [(C_OUT, MID), (3, 3, MID, MID), (MID, C_OUT)]

def pieces(flat_array, bounds, shapes):
    return [flat_array[bounds[ordinal]:bounds[ordinal + 1]].reshape(shapes[ordinal]) for ordinal in range(len(shapes))]

def matmul(left, right):
    return jnp.dot(left, right, precision=lax.Precision.HIGHEST, preferred_element_type=jnp.float32)

def pointwise(images, weight):
    return matmul(images.reshape(-1, images.shape[-1]), weight).reshape(images.shape[:-1] + (weight.shape[1],))

def windows(images, stride):
    number, in_side, _, channels = images.shape
    out_side = in_side // stride
    padded = jnp.pad(images, ((0, 0), (1, 1), (1, 1), (0, 0)))
    span_out = stride * (out_side - 1) + 1
    result = []
    for row_tap in range(3):
        for col_tap in range(3):
            result.append(lax.slice(padded, (0, row_tap, col_tap, 0), (number, row_tap + span_out, col_tap + span_out, channels), (1, stride, stride, 1)))
    return result

def conv_three(images, weight, stride):
    number, in_side, _, channels = images.shape
    out_side = in_side // stride
    summed = jnp.zeros((number * out_side * out_side, weight.shape[3]), jnp.float32)
    for position, window in enumerate(windows(images, stride)):
        summed = summed + matmul(window.reshape(-1, channels), weight[position // 3, position % 3])
    return summed.reshape(number, out_side, out_side, weight.shape[3])

def norm_layer(tensors, present, affine):
    summed = jnp.zeros((tensors[0].shape[-1],), jnp.float32)
    squares = jnp.zeros((tensors[0].shape[-1],), jnp.float32)
    pixels = jnp.zeros((), jnp.float32)
    for tensor, marker in zip(tensors, present):
        weighted = tensor * marker[:, None, None, None]
        summed = summed + lax.optimization_barrier(jnp.sum(weighted, axis=(0, 1, 2)))
        squares = squares + lax.optimization_barrier(jnp.sum(weighted * tensor, axis=(0, 1, 2)))
        pixels = pixels + jnp.sum(marker) * (tensor.shape[1] * tensor.shape[2])
    center = summed / pixels
    variance = squares / pixels - center * center
    factor = lax.rsqrt(variance + EPSILON)
    return [(tensor - center) * factor * affine[0] + affine[1] for tensor in tensors]

def forward(parameters, images, present):
    weights_a, weights_b, gains_narrow, gains_wide = parameters
    reduce_a, spatial_a, expand_a, project_a = pieces(low(weights_a), bounds_a(), shapes_a())
    reduce_b, spatial_b, expand_b = pieces(low(weights_b), bounds_b(), shapes_b())
    pre_one = [low_back(pointwise(picture, reduce_a)) for picture in images]
    act_one = [low(jax.nn.silu(tensor)) for tensor in norm_layer(pre_one, present, gains_narrow[0])]
    pre_two = [low_back(conv_three(tensor, spatial_a, 2)) for tensor in act_one]
    act_two = [low(jax.nn.silu(tensor)) for tensor in norm_layer(pre_two, present, gains_narrow[1])]
    pre_main = [low_back(pointwise(tensor, expand_a)) for tensor in act_two]
    pre_side = [low_back(pointwise(picture[:, ::2, ::2, :], project_a)) for picture in images]
    branch_out = norm_layer(pre_main, present, gains_wide[0])
    bypass_out = norm_layer(pre_side, present, gains_wide[1])
    middle = [low(jax.nn.silu(branch + bypass)) for branch, bypass in zip(branch_out, bypass_out)]
    pre_four = [low_back(pointwise(tensor, reduce_b)) for tensor in middle]
    act_four = [low(jax.nn.silu(tensor)) for tensor in norm_layer(pre_four, present, gains_narrow[2])]
    pre_five = [low_back(conv_three(tensor, spatial_b, 1)) for tensor in act_four]
    act_five = [low(jax.nn.silu(tensor)) for tensor in norm_layer(pre_five, present, gains_narrow[3])]
    pre_six = [low_back(pointwise(tensor, expand_b)) for tensor in act_five]
    out_six = norm_layer(pre_six, present, gains_wide[2])
    return [jax.nn.silu(tensor + residual) for tensor, residual in zip(out_six, middle)]

def group_gradients(parameters, images, cotangents, group_counts):
    present = []
    for column in range(3):
        slots = images[column].shape[0] // N_GX
        marker = jnp.arange(slots, dtype=jnp.int32)[None, :] < group_counts[:, column][:, None]
        present.append(marker.reshape(-1).astype(jnp.float32))
    outputs, pullback = jax.vjp(partial(forward, present=present), parameters, images)
    targets = [cotangent * marker[:, None, None, None] for cotangent, marker in zip(cotangents, present)]
    return pullback(targets)

def regroup(array):
    shape = array.shape
    slots = shape[0] // (N_GX * N_GY)
    reshaped = array.reshape((N_GX, N_GY, slots) + shape[1:]).swapaxes(0, 1)
    return reshaped.reshape((N_GY, N_GX * slots) + shape[1:])

def ungroup(array):
    shape = array.shape
    slots = shape[1] // N_GX
    reshaped = array.reshape((N_GY, N_GX, slots) + shape[2:]).swapaxes(0, 1)
    return reshaped.reshape((N_GX * N_GY * slots,) + shape[2:])

def lars_update(weights, moment, gradients, bounds):
    updates = []
    layer_norms = []
    for layer_index in range(len(bounds) - 1):
        weight_part = weights[bounds[layer_index]:bounds[layer_index + 1]]
        grad_part = gradients[bounds[layer_index]:bounds[layer_index + 1]]
        weight_norm = jnp.sqrt(jnp.sum(weight_part * weight_part))
        grad_norm = jnp.sqrt(jnp.sum(grad_part * grad_part))
        trust_ratio = TRUST_SCALE * weight_norm / (grad_norm + WEIGHT_DECAY * weight_norm)
        updates.append(LEARN_RATE * trust_ratio * (grad_part + WEIGHT_DECAY * weight_part))
        layer_norms.append(jnp.stack([weight_norm, grad_norm]))
    new_moment = MOMENTUM * moment + jnp.concatenate(updates)
    return (new_moment, layer_norms)

def reference(image_small, image_medium, image_large, cot_small, cot_medium, cot_large, counts, weights_a, weights_b, moment_a, moment_b, gains_narrow, gains_wide, gain_moment_narrow, gain_moment_wide):
    images = tuple((regroup(picture.astype(jnp.float32)) for picture in (image_small, image_medium, image_large)))
    cotangents = tuple((regroup(cotangent.astype(jnp.float32)) for cotangent in (cot_small, cot_medium, cot_large)))
    grouped_counts = counts.reshape(N_GX, N_GY, 3).swapaxes(0, 1)
    parameters = (weights_a, weights_b, gains_narrow, gains_wide)
    start = jax.tree.map(lambda leaf: jnp.zeros(leaf.shape, jnp.float32), parameters)

    def group_step(carried, slices):
        group_images, group_cots, group_counts = slices
        param_grads, image_grads = group_gradients(parameters, list(group_images), list(group_cots), group_counts)
        carried = jax.tree.map(lambda total_leaf, new_leaf: total_leaf + new_leaf, carried, param_grads)
        return (carried, tuple((gradient.astype(jnp.bfloat16) for gradient in image_grads)))
    totals, image_grads = lax.scan(group_step, start, (images, cotangents, grouped_counts))
    sides = [O_S, O_M, O_L]
    pixels_total = jnp.zeros((), jnp.float32)
    for column in range(3):
        pixels_total = pixels_total + jnp.sum(counts[:, column].astype(jnp.float32)) * (sides[column] * sides[column])
    grad_a = totals[0] / pixels_total
    grad_b = totals[1] / pixels_total
    new_moment_a, norms_a = lars_update(weights_a, moment_a, grad_a, bounds_a())
    new_moment_b, norms_b = lars_update(weights_b, moment_b, grad_b, bounds_b())
    new_gain_moment_narrow = MOMENTUM * gain_moment_narrow + GAIN_RATE * (totals[2] / pixels_total)
    new_gain_moment_wide = MOMENTUM * gain_moment_wide + GAIN_RATE * (totals[3] / pixels_total)
    layer_norms = jnp.stack(norms_a + norms_b)
    return (ungroup(image_grads[0]), ungroup(image_grads[1]), ungroup(image_grads[2]), new_moment_a, new_moment_b, new_gain_moment_narrow, new_gain_moment_wide, layer_norms)
```

```python
import functools

import jax
import jax.numpy as jnp
import numpy as np
from jax import lax
from jax.experimental import pallas as pl
from jax.experimental.pallas import tpu as pltpu
from jax.sharding import PartitionSpec as P

C_IN = 1024
MID = 512
C_OUT = 2048

EPSILON = 1e-05
MOMENTUM = 0.9
LEARN_RATE = 20.0
TRUST_SCALE = 0.001
WEIGHT_DECAY = 5e-05
GAIN_RATE = 0.2

MESH = pl.DeviceIdType.MESH
F32 = jnp.float32
BF16 = jnp.bfloat16
TILE = 256
ROWS = 64
WIDE = C_OUT // MID

ROW_RA, ROW_SA, ROW_EA, ROW_PA = 0, C_IN, C_IN + 9 * MID, C_IN + 9 * MID + C_OUT
END_A = ROW_PA + C_IN * WIDE
ROW_RB, ROW_SB, ROW_EB = 0, C_OUT, C_OUT + 9 * MID
END_B = ROW_EB + C_OUT

EXCHANGES = 12


def round_up(value, unit):
    return -(-value // unit) * unit


class Layout:
    def __init__(self, shapes):
        pictures = [
            (shape[1] // 2, res, slot)
            for res, shape in enumerate(shapes)
            for slot in range(shape[0])
        ]
        pictures.sort(key=lambda item: (-item[0], item[2]))
        self.tiles = []
        self.fill = []
        for side, res, slot in pictures:
            for tile in range(len(self.tiles) + 1):
                if tile == len(self.tiles):
                    self.tiles.append([])
                    self.fill.append(0)
                if self.fill[tile] + side * side <= TILE:
                    self.tiles[tile].append((side, res, slot, self.fill[tile]))
                    self.fill[tile] += side * side
                    break
        self.rows = TILE * len(self.tiles)

    def where(self):
        res_of = np.zeros((self.rows, 1), np.int32)
        slot_of = np.full((self.rows, 1), 1 << 20, np.int32)
        for tile, members in enumerate(self.tiles):
            for side, res, slot, start in members:
                first = tile * TILE + start
                res_of[first : first + side * side] = res
                slot_of[first : first + side * side] = slot
        return res_of, slot_of

    def neighbours(self):
        table = np.full((16, self.rows), -1, np.int32)
        for tap in range(9):
            down, right = tap // 3 - 1, tap % 3 - 1
            for tile, members in enumerate(self.tiles):
                for side, _, _, start in members:
                    for i in range(side):
                        for j in range(side):
                            if 0 <= i + down < side and 0 <= j + right < side:
                                table[tap, tile * TILE + start + i * side + j] = (
                                    start + (i + down) * side + j + right
                                )
        return table

    def picture_rows(self, side_of):
        result = []
        for members in self.tiles:
            codes = []
            for side, _, _, start in members:
                full = side_of(side)
                step = full // side
                padded = round_up(full, 16)
                code = np.full((full, padded), -1, np.int32)
                for r in range(full):
                    for c in range(full):
                        kind = (r % step) * 2 + (c % step)
                        code[r, c] = kind * TILE + start + (r // step) * side + c // step
                codes.append(code.reshape(1, -1))
            result.append(codes)
        return result

    def picture_back(self):
        result = []
        for members in self.tiles:
            for side, _, _, start in members:
                full = 2 * side
                padded = round_up(full, 16)
                back = np.full((4 * TILE,), -1, np.int32)
                for r in range(full):
                    for c in range(full):
                        kind = (r % 2) * 2 + (c % 2)
                        back[kind * TILE + start + (r // 2) * side + c // 2] = r * padded + c
                result.append(back)
        return np.stack(result)


def dot(left, right):
    return jnp.dot(left, right, preferred_element_type=F32)


def dot_tn(left, right):
    return lax.dot_general(left, right, (((0,), (0,)), ((), ())), preferred_element_type=F32)


def dot_nt(left, right):
    return lax.dot_general(left, right, (((1,), (1,)), ((), ())), preferred_element_type=F32)


def sigmoid(value):
    return 0.5 * jnp.tanh(0.5 * value) + 0.5


def one_hot(targets, count, offset=0):
    ids = lax.broadcasted_iota(jnp.int32, (count, targets.shape[1]), 0) + offset
    return jnp.where(ids == targets, 1.0, 0.0).astype(BF16)


def loop(count, body, unroll=1):
    def step(index, carry):
        body(index)
        return carry

    lax.fori_loop(0, count, step, 0, unroll=unroll)


def columns(index, width=MID):
    if isinstance(index, int):
        return pl.ds(index * width, width)
    return pl.ds(pl.multiple_of(index * width, width), width)


def mega(
    layout,
    groups,
    img_s,
    img_m,
    img_l,
    cot_s,
    cot_m,
    cot_l,
    wa,
    wb,
    mask,
    pixels,
    gains_n,
    gains_w,
    shifts,
    codes_img,
    codes_cot,
    codes_back,
    out_s,
    out_m,
    out_l,
    dwa,
    dwb,
    totals,
    z_one,
    z_main,
    z_side,
    z_six,
    g_wide,
    middle,
    cot_p,
    gp_side,
    act_one,
    z_two,
    z_four,
    z_five,
    g_nar,
    act_two,
    act_four,
    act_five,
    gp_nar,
    shifted,
    x_p,
    w_ra,
    w_sp,
    w_ea,
    w_pa,
    w_rb,
    w_eb,
    w_raw,
    d_acc,
    d_out,
    stats,
    arrived,
    par,
    wsem,
    rsem,
    dsem,
    isem,
    xsend,
    xrecv,
):
    rows = layout.rows
    tiles = len(layout.tiles)
    steps = rows // ROWS
    me_x = lax.axis_index("gx")
    me_y = lax.axis_index("gy")

    barrier = pltpu.get_barrier_semaphore()
    for hop in range(1, groups):
        pl.semaphore_signal(
            barrier,
            inc=1,
            device_id=(lax.rem(me_x + hop, groups), me_y),
            device_id_type=MESH,
        )

    def fetch(source, first, count, target, sem):
        return pltpu.make_async_copy(source.at[pl.ds(first, count)], target, wsem.at[sem])

    get_ra = fetch(wa, ROW_RA, C_IN, w_ra, 0)
    get_sa = fetch(wa, ROW_SA, 9 * MID, w_sp, 1)
    get_rb = fetch(wb, ROW_RB, C_OUT, w_rb, 2)
    get_sb = fetch(wb, ROW_SB, 9 * MID, w_sp, 3)
    get_ra.start()
    get_sa.start()
    get_rb.start()

    def unravel(source, first, count, target):
        chunks = count * WIDE // TILE
        part = TILE // WIDE

        def raw(chunk):
            slot = lax.rem(chunk, 2)
            return pltpu.make_async_copy(
                source.at[pl.ds(pl.multiple_of(first + chunk * TILE, TILE), TILE)],
                w_raw.at[slot],
                rsem.at[slot],
            )

        raw(0).start()
        lane = lax.broadcasted_iota(jnp.int32, (1, TILE), 1)
        order = one_hot(lax.rem(lane, WIDE) * part + lax.div(lane, WIDE), TILE)

        def body(chunk):
            @pl.when(chunk + 1 < chunks)
            def _():
                raw(chunk + 1).start()

            raw(chunk).wait()
            sorted_rows = dot(order, w_raw[lax.rem(chunk, 2)]).astype(BF16)
            where = pl.ds(pl.multiple_of(chunk * part, part), part)
            for k in range(WIDE):
                target[where, k * MID : (k + 1) * MID] = sorted_rows[k * part : (k + 1) * part]

        loop(chunks, body)

    def gather_pictures(refs, codes, side_of, kinds, width, target):
        at = 0
        for tile, members in enumerate(layout.tiles):
            shapes = [(side_of(side), round_up(side_of(side), 16)) for side, _, _, _ in members]

            def scoped(*buffers, tile=tile, members=members, shapes=shapes, at=at):
                raws, pads = buffers[: len(members)], buffers[len(members) :]
                copies = [
                    pltpu.make_async_copy(refs[res].at[slot], raws[k], isem.at[k])
                    for k, (_, res, slot, _) in enumerate(members)
                ]
                for copy in copies:
                    copy.start()
                for k, (full, padded) in enumerate(shapes):
                    pads[k][...] = jnp.zeros(pads[k].shape, BF16)
                    copies[k].wait()
                    pads[k][:, :full, :] = raws[k][...]
                blocks = width // MID

                def body(index):
                    kind, block = index // blocks, lax.rem(index, blocks)
                    total = None
                    for k, (full, padded) in enumerate(shapes):
                        count = full * padded
                        lanes = codes[at + k : at + k + 1, :count]
                        data = pads[k][:, :, columns(block)].reshape(count, MID)
                        term = dot(one_hot(lanes, TILE, kind * TILE), data)
                        total = term if total is None else total + term
                    target[
                        tile * TILE : (tile + 1) * TILE, columns(kind * blocks + block)
                    ] = total.astype(BF16)

                loop(kinds * blocks, body)

            pl.run_scoped(
                scoped,
                *[pltpu.VMEM((full, full, width), BF16) for full, _ in shapes],
                *[pltpu.VMEM((full, padded, width), BF16) for full, padded in shapes],
            )
            at += len(members)

    gather_pictures((img_s, img_m, img_l), codes_img, lambda side: 2 * side, 4, C_IN, x_p)
    gather_pictures((cot_s, cot_m, cot_l), codes_cot, lambda side: side, 1, C_OUT, cot_p)

    pl.semaphore_wait(barrier, groups - 1)

    def copies_of(e, count):
        return [
            pltpu.make_async_remote_copy(
                src_ref=stats.at[e, pl.ds(0, count)],
                dst_ref=arrived.at[e, me_x, pl.ds(0, count)],
                send_sem=xsend.at[e, hop - 1],
                recv_sem=xrecv.at[e, hop - 1],
                device_id=(lax.rem(me_x + hop, groups), me_y),
                device_id_type=MESH,
            )
            for hop in range(1, groups)
        ]

    def send(e, count):
        for copy in copies_of(e, count):
            copy.start()
        arrived[e, pl.ds(me_x, 1), :count] = stats[e : e + 1, :count]

    def receive(e, count):
        for copy in copies_of(e, count):
            copy.wait()
        total = arrived[e, 0, :count]
        for other in range(1, groups):
            total = total + arrived[e, other, :count]
        totals[e, :count] = total

    def clear(e):
        stats[e] = jnp.zeros(stats.shape[1:], F32)

    def each(width, body):
        def step(index):
            block, step_row = index // steps, lax.rem(index, steps)
            body(pl.ds(pl.multiple_of(step_row * ROWS, ROWS), ROWS), block)

        loop(width * steps, step, unroll=2)

    def each_sums(width, body, e, targets):
        def block_step(block):
            def step(index, carry):
                values = body(pl.ds(pl.multiple_of(index * ROWS, ROWS), ROWS), block)
                return tuple(
                    kept + jnp.sum(value.reshape(ROWS // 8, 8, MID), axis=0)
                    for kept, value in zip(carry, values)
                )

            start = tuple(jnp.zeros((8, MID), F32) for _ in targets(0))
            sums = lax.fori_loop(0, steps, step, start, unroll=2)
            for row, value in zip(targets(block), sums):
                stats[e, pl.ds(row, 1)] += jnp.sum(value, axis=0, keepdims=True)

        loop(width, block_step)

    def moments(source, e, width, same=False, first=0):
        def body(here, block):
            value = source[here, columns(block)].astype(F32)
            kept = value * mask[here, :]
            return kept, kept * value

        if same:
            each_sums(width, body, e, lambda block: (first, first + 1))
        else:
            each_sums(width, body, e, lambda block: (first + block, first + width + block))

    def pixel_row():
        return totals[0, 2:3]

    def coefficients(e, first, width, gain_rows, k, pixel_scale):
        count = pixel_row() * pixel_scale
        for j in range(width):
            center = totals[e, first + j : first + j + 1] / count
            square = totals[e, first + width + j : first + width + j + 1] / count
            factor = lax.rsqrt(square - center * center + EPSILON)
            gain, offset = gain_rows(j)
            scale = gain * factor
            par[k, j : j + 1] = scale
            par[k, width + j : width + j + 1] = offset - center * scale
            par[k, 2 * width + j : 2 * width + j + 1] = factor
            par[k, 3 * width + j : 3 * width + j + 1] = -center * factor

    def narrow_gains(k):
        return lambda j: (gains_n[k, 0:1, :], gains_n[k, 1:2, :])

    def wide_gains(k):
        return lambda j: (
            gains_w[k, 0:1, j * MID : (j + 1) * MID],
            gains_w[k, 1:2, j * MID : (j + 1) * MID],
        )

    def row_of(k, which, width, block):
        return par[k, pl.ds(which * width + block, 1)]

    def back_coefficients(e, sum_first, cross_first, width, k, pixel_scale):
        count = pixel_row() * pixel_scale
        for j in range(width):
            total_g = totals[e, sum_first + j : sum_first + j + 1]
            total_x = totals[e, cross_first + j : cross_first + j + 1]
            scale = par[k, j : j + 1]
            factor = par[k, 2 * width + j : 2 * width + j + 1]
            shift = par[k, 3 * width + j : 3 * width + j + 1]
            par[k + 8, j : j + 1] = scale * (total_g + shift * total_x) / count
            par[k + 8, width + j : width + j + 1] = scale * factor * total_x / count

    def activate(source, target, k):
        def body(here, block):
            value = source[here, columns(block)].astype(F32)
            value = value * row_of(k, 0, 1, 0) + row_of(k, 1, 1, 0)
            target[here, columns(block)] = (value * sigmoid(value)).astype(BF16)

        each(source.shape[1] // MID, body)

    def slope(value):
        s = sigmoid(value)
        return s * (1.0 + value * (1.0 - s))

    def back_activate(grad, source, k, e, same=False):
        def body(here, block):
            z = source[here, columns(block)].astype(F32)
            g = grad[here, columns(block)] * slope(z * row_of(k, 0, 1, 0) + row_of(k, 1, 1, 0))
            grad[here, columns(block)] = g
            return g, g * (z * row_of(k, 2, 1, 0) + row_of(k, 3, 1, 0))

        each_sums(source.shape[1] // MID, body, e, lambda block: (0, 1))

    def back_norm(grad, source, target, k, width, same=False):
        def body(here, block):
            j = 0 if same else block
            z = source[here, columns(block)].astype(F32)
            g = grad[here, columns(block)]
            fixed = row_of(k + 8, 0, width, j) + z * row_of(k + 8, 1, width, j)
            value = g * row_of(k, 0, width, j) - mask[here, :] * fixed
            target[here, columns(block)] = value.astype(BF16)

        each(source.shape[1] // MID, body)

    def shift_into(source, block, table_row, target):
        for tile in range(tiles):
            here = slice(tile * TILE, (tile + 1) * TILE)
            pick = one_hot(shifts[pl.ds(table_row, 1), here], TILE)
            target[here, :] = dot(pick, source[here, columns(block)]).astype(BF16)

    def strided_tap(tap):
        p, q = tap // 3, lax.rem(tap, 3)
        kind = 2 * lax.rem(p + 1, 2) + lax.rem(q + 1, 2)
        return kind, ((p + 1) // 2) * 3 + (q + 1) // 2

    def tap_weight(tap):
        return w_sp[columns(tap), :]

    clear_all = jnp.zeros(stats.shape[1:], F32)
    for e in range(EXCHANGES):
        stats[e] = clear_all

    get_ra.wait()

    def first_product(kind):
        z_one[:, columns(kind)] = dot(x_p[:, columns(kind, C_IN)], w_ra[...])

    loop(4, first_product)
    moments(z_one, 0, 4, same=True)
    stats[0, 2:3] = pixels[...]
    send(0, 8)
    unravel(wa, ROW_EA, MID, w_ea)
    unravel(wa, ROW_PA, C_IN, w_pa)
    receive(0, 8)
    coefficients(0, 0, 1, narrow_gains(0), 0, 4.0)
    activate(z_one, act_one, 0)

    get_sa.wait()
    z_two[...] = jnp.zeros(z_two.shape, F32)

    def conv_a(tap):
        kind, table_row = strided_tap(tap)
        shift_into(act_one, kind, 8 - table_row, shifted)
        z_two[...] += dot(shifted[...], tap_weight(tap))

    loop(9, conv_a)
    get_sb.start()
    moments(z_two, 1, 1)
    send(1, 8)

    def side_product(block):
        z_side[:, columns(block)] = dot(x_p[:, :C_IN], w_pa[:, columns(block)]).astype(z_side.dtype)

    loop(WIDE, side_product)
    moments(z_side, 2, WIDE, first=8)
    receive(1, 8)
    coefficients(1, 0, 1, narrow_gains(1), 1, 1.0)
    activate(z_two, act_two, 1)

    def main_product(block):
        z_main[:, columns(block)] = dot(act_two[...], w_ea[:, columns(block)]).astype(z_main.dtype)

    loop(WIDE, main_product)
    moments(z_main, 2, WIDE)
    send(2, 16)
    unravel(wb, ROW_EB, MID, w_eb)
    receive(2, 16)
    coefficients(2, 0, WIDE, wide_gains(0), 4, 1.0)
    coefficients(2, 8, WIDE, wide_gains(1), 5, 1.0)

    def joined_a(here, block):
        main = z_main[here, columns(block)].astype(F32)
        side = z_side[here, columns(block)].astype(F32)
        value = main * row_of(4, 0, WIDE, block) + row_of(4, 1, WIDE, block)
        return main, side, value + side * row_of(5, 0, WIDE, block) + row_of(5, 1, WIDE, block)

    def middle_step(here, block):
        _, _, value = joined_a(here, block)
        middle[here, columns(block)] = (value * sigmoid(value)).astype(BF16)

    each(WIDE, middle_step)
    get_rb.wait()
    z_four[...] = dot(middle[...], w_rb[...])
    moments(z_four, 3, 1)
    send(3, 8)
    receive(3, 8)
    coefficients(3, 0, 1, narrow_gains(2), 2, 1.0)
    activate(z_four, act_four, 2)

    get_sb.wait()
    z_five[...] = jnp.zeros(z_five.shape, F32)

    def conv_b(tap):
        shift_into(act_four, 0, 8 - tap, shifted)
        z_five[...] += dot(shifted[...], tap_weight(tap))

    loop(9, conv_b)
    moments(z_five, 4, 1)
    send(4, 8)
    receive(4, 8)
    coefficients(4, 0, 1, narrow_gains(3), 3, 1.0)
    activate(z_five, act_five, 3)

    def last_product(block):
        z_six[:, columns(block)] = dot(act_five[...], w_eb[:, columns(block)]).astype(z_six.dtype)

    loop(WIDE, last_product)
    moments(z_six, 5, WIDE)
    send(5, 8)
    receive(5, 8)
    coefficients(5, 0, WIDE, wide_gains(2), 6, 1.0)

    def output_step(here, block):
        z = z_six[here, columns(block)].astype(F32)
        value = z * row_of(6, 0, WIDE, block) + row_of(6, 1, WIDE, block)
        value = value + middle[here, columns(block)].astype(F32)
        g = cot_p[here, columns(block)].astype(F32) * mask[here, :] * slope(value)
        g_wide[here, columns(block)] = g
        return g, g * (z * row_of(6, 2, WIDE, block) + row_of(6, 3, WIDE, block))

    each_sums(WIDE, output_step, 6, lambda block: (block, WIDE + block))
    send(6, 8)
    receive(6, 8)
    back_coefficients(6, 0, WIDE, WIDE, 6, 1.0)
    gp_six = cot_p
    back_norm(g_wide, z_six, gp_six, 6, WIDE)

    def put(unit, first, target, slot):
        return pltpu.make_async_copy(
            d_out.at[slot],
            target.at[pl.ds(pl.multiple_of(first + unit * MID, MID), MID)],
            dsem.at[slot],
        )

    def store_unit(unit, first, target, value):
        slot = lax.rem(unit, 2) if not isinstance(unit, int) else unit % 2

        @pl.when(unit >= 2)
        def _():
            put(unit, first, target, slot).wait()

        d_out[slot] = value.astype(BF16)
        put(unit, first, target, slot).start()

    def flush(first, target):
        for slot in range(2):
            put(0, first, target, slot).wait()

    def wide_weight_grad(left, left_count, grad, first, target):
        def body(chunk):
            part = left[:, columns(chunk, TILE)]
            for k in range(WIDE):
                value = dot_tn(part, grad[:, columns(k)])
                for lane in range(MID // 128):
                    d_acc[lane, pl.ds(k, TILE, stride=WIDE), :] = value[:, lane * 128 : (lane + 1) * 128]
            for half in range(2):
                here = slice(half * MID, (half + 1) * MID)
                value = jnp.concatenate([d_acc[lane, here] for lane in range(MID // 128)], axis=1)
                store_unit(chunk * 2 + half, first, target, value)

        loop(left_count // TILE, body)
        flush(first, target)

    g_nar[...] = dot_nt(gp_six[...], w_eb[...])
    back_activate(g_nar, z_five, 3, 7)
    send(7, 8)
    wide_weight_grad(act_five, MID, gp_six, ROW_EB, dwb)
    receive(7, 8)
    back_coefficients(7, 0, 1, 1, 3, 1.0)
    back_norm(g_nar, z_five, gp_nar, 3, 1)

    g_nar[...] = jnp.zeros(g_nar.shape, F32)

    def conv_b_back(tap):
        shift_into(gp_nar, 0, tap, shifted)
        g_nar[...] += dot_nt(shifted[...], tap_weight(tap))
        store_unit(tap, ROW_SB, dwb, dot_tn(act_four[...], shifted[...]))

    loop(9, conv_b_back)
    get_sa.start()
    back_activate(g_nar, z_four, 2, 8)
    send(8, 8)
    flush(ROW_SB, dwb)
    receive(8, 8)
    back_coefficients(8, 0, 1, 1, 2, 1.0)
    back_norm(g_nar, z_four, gp_nar, 2, 1)

    def middle_back(block):
        g_wide[:, columns(block)] += dot_nt(gp_nar[...], w_rb[columns(block), :])

    loop(WIDE, middle_back)

    def join_step(here, block):
        main, side, value = joined_a(here, block)
        g = g_wide[here, columns(block)] * slope(value)
        g_wide[here, columns(block)] = g
        return (
            g,
            g * (main * row_of(4, 2, WIDE, block) + row_of(4, 3, WIDE, block)),
            g * (side * row_of(5, 2, WIDE, block) + row_of(5, 3, WIDE, block)),
        )

    each_sums(WIDE, join_step, 9, lambda block: (block, WIDE + block, 2 * WIDE + block))
    send(9, 16)

    def reduce_b_grad(block):
        store_unit(block, ROW_RB, dwb, dot_tn(middle[:, columns(block)], gp_nar[...]))

    loop(WIDE, reduce_b_grad)
    flush(ROW_RB, dwb)
    receive(9, 16)
    back_coefficients(9, 0, WIDE, WIDE, 4, 1.0)
    back_coefficients(9, 0, 2 * WIDE, WIDE, 5, 1.0)
    gp_main = cot_p
    back_norm(g_wide, z_main, gp_main, 4, WIDE)
    back_norm(g_wide, z_side, gp_side, 5, WIDE)

    g_nar[...] = dot_nt(gp_main[...], w_ea[...])
    back_activate(g_nar, z_two, 1, 10)
    send(10, 8)
    wide_weight_grad(act_two, MID, gp_main, ROW_EA, dwa)
    receive(10, 8)
    back_coefficients(10, 0, 1, 1, 1, 1.0)
    back_norm(g_nar, z_two, gp_nar, 1, 1)

    get_sa.wait()
    g_one = g_wide
    g_one[...] = jnp.zeros(g_one.shape, F32)

    def conv_a_back(tap):
        kind, table_row = strided_tap(tap)
        shift_into(gp_nar, 0, table_row, shifted)
        g_one[:, columns(kind)] += dot_nt(shifted[...], tap_weight(tap))
        store_unit(tap, ROW_SA, dwa, dot_tn(act_one[:, columns(kind)], shifted[...]))

    loop(9, conv_a_back)
    back_activate(g_one, z_one, 0, 11)
    send(11, 8)
    flush(ROW_SA, dwa)
    wide_weight_grad(x_p, C_IN, gp_side, ROW_PA, dwa)
    receive(11, 8)
    back_coefficients(11, 0, 1, 1, 0, 4.0)
    gp_one = act_one
    back_norm(g_one, z_one, gp_one, 0, 1, same=True)

    for half in range(C_IN // MID):
        total = None
        for kind in range(4):
            left = x_p[:, kind * C_IN + half * MID : kind * C_IN + (half + 1) * MID]
            term = dot_tn(left, gp_one[:, columns(kind)])
            total = term if total is None else total + term
        store_unit(half, ROW_RA, dwa, total)

    def image_back(kind):
        value = dot_nt(gp_one[:, columns(kind)], w_ra[...])
        x_p[:, columns(kind, C_IN)] = value.astype(BF16)

    x_side = dot_nt(gp_one[:, :MID], w_ra[...]) + dot_nt(gp_side[...], w_pa[...])
    x_p[:, :C_IN] = x_side.astype(BF16)
    for kind in range(1, 4):
        image_back(kind)
    flush(ROW_RA, dwa)

    outs = (out_s, out_m, out_l)
    at = 0
    for tile, members in enumerate(layout.tiles):
        shapes = [(2 * side, round_up(2 * side, 16)) for side, _, _, _ in members]

        def scoped(*raws, tile=tile, members=members, shapes=shapes, at=at):
            here = slice(tile * TILE, (tile + 1) * TILE)
            copies = []
            for k, (full, padded) in enumerate(shapes):
                count = full * padded
                for block in range(C_IN // MID):
                    total = None
                    for kind in range(4):
                        lanes = codes_back[at + k : at + k + 1, kind * TILE : (kind + 1) * TILE]
                        data = x_p[here, kind * C_IN + block * MID : kind * C_IN + (block + 1) * MID]
                        term = dot(one_hot(lanes, count), data)
                        total = term if total is None else total + term
                    total = total.astype(BF16).reshape(full, padded, MID)
                    raws[k][:, :, block * MID : (block + 1) * MID] = total[:, :full, :]
                _, res, slot, _ = members[k]
                copy = pltpu.make_async_copy(raws[k], outs[res].at[slot], isem.at[k])
                copy.start()
                copies.append(copy)
            for copy in copies:
                copy.wait()

        pl.run_scoped(scoped, *[pltpu.VMEM((full, full, C_IN), BF16) for full, _ in shapes])
        at += len(members)


def both_blocks(groups, images, cots, wa, wb, mask, pixels, gains_narrow, gains_wide):
    layout = Layout([image.shape for image in images])
    rows = layout.rows
    img_codes = [code for tile in layout.picture_rows(lambda side: 2 * side) for code in tile]
    cot_codes = [code for tile in layout.picture_rows(lambda side: side) for code in tile]

    def table(codes):
        width = round_up(max(code.shape[1] for code in codes), 128)
        result = np.full((round_up(len(codes), 8), width), -1, np.int32)
        for index, code in enumerate(codes):
            result[index, : code.shape[1]] = code[0]
        return jnp.asarray(result)

    back = layout.picture_back()
    back = np.concatenate([back, np.full((round_up(len(back), 8) - len(back), back.shape[1]), -1, np.int32)])
    members = max(len(tile) for tile in layout.tiles)
    anywhere = pl.BlockSpec(memory_space=pl.ANY)
    vmem = pl.BlockSpec(memory_space=pltpu.VMEM)
    wide16 = pltpu.VMEM((rows, C_OUT), BF16)
    wide32 = pltpu.VMEM((rows, C_OUT), F32)
    nar16 = pltpu.VMEM((rows, MID), BF16)
    nar32 = pltpu.VMEM((rows, MID), F32)
    return pl.pallas_call(
        functools.partial(mega, layout, groups),
        out_shape=(
            *[jax.ShapeDtypeStruct(image.shape, BF16) for image in images],
            jax.ShapeDtypeStruct((END_A, MID), BF16),
            jax.ShapeDtypeStruct((END_B, MID), BF16),
            jax.ShapeDtypeStruct((EXCHANGES, 16, MID), F32),
        ),
        in_specs=[anywhere] * 8 + [vmem] * 8,
        out_specs=(anywhere,) * 5 + (vmem,),
        scratch_shapes=[
            wide32,
            wide16,
            wide16,
            wide16,
            wide32,
            wide16,
            wide16,
            wide16,
            wide16,
            nar32,
            nar32,
            nar32,
            nar32,
            nar16,
            nar16,
            nar16,
            nar16,
            nar16,
            pltpu.VMEM((rows, 4 * C_IN), BF16),
            pltpu.VMEM((C_IN, MID), BF16),
            pltpu.VMEM((9 * MID, MID), BF16),
            pltpu.VMEM((MID, C_OUT), BF16),
            pltpu.VMEM((C_IN, C_OUT), BF16),
            pltpu.VMEM((C_OUT, MID), BF16),
            pltpu.VMEM((MID, C_OUT), BF16),
            pltpu.VMEM((2, TILE, MID), BF16),
            pltpu.VMEM((MID // 128, WIDE * TILE, 128), F32),
            pltpu.VMEM((2, MID, MID), BF16),
            pltpu.VMEM((EXCHANGES, 16, MID), F32),
            pltpu.VMEM((EXCHANGES, groups, 16, MID), F32),
            pltpu.VMEM((16, 16, MID), F32),
            pltpu.SemaphoreType.DMA((4,)),
            pltpu.SemaphoreType.DMA((2,)),
            pltpu.SemaphoreType.DMA((2,)),
            pltpu.SemaphoreType.DMA((members,)),
            pltpu.SemaphoreType.DMA((EXCHANGES, groups - 1)),
            pltpu.SemaphoreType.DMA((EXCHANGES, groups - 1)),
        ],
        compiler_params=pltpu.CompilerParams(
            collective_id=0, has_side_effects=True, vmem_limit_bytes=63 * 1024 * 1024
        ),
    )(
        *images,
        *cots,
        wa,
        wb,
        mask,
        pixels,
        gains_narrow,
        gains_wide,
        jnp.asarray(layout.neighbours()),
        table(img_codes),
        table(cot_codes),
        jnp.asarray(back),
    )


def layer_masks(first, count, bounds):
    position = first + jnp.arange(count, dtype=jnp.int32)
    rows = [(position >= low) & (position < high) for low, high in zip(bounds[:-1], bounds[1:])]
    return jnp.stack(rows).astype(F32)


def body(
    image_small,
    image_medium,
    image_large,
    cot_small,
    cot_medium,
    cot_large,
    counts,
    weights_a,
    weights_b,
    moment_a,
    moment_b,
    gains_narrow,
    gains_wide,
    gain_moment_narrow,
    gain_moment_wide,
):
    images = (image_small, image_medium, image_large)
    cots = (cot_small, cot_medium, cot_large)
    groups = lax.axis_size("gx")
    layout = Layout([image.shape for image in images])
    res_of, slot_of = layout.where()
    limit = sum(jnp.where(res_of == r, counts[0, r], 0) for r in range(3))
    mask = (slot_of < limit).astype(F32)
    local_pixels = jnp.sum(mask)
    rows_a = weights_a.shape[0] // MID
    rows_b = weights_b.shape[0] // MID
    flat_a = weights_a.reshape(rows_a, MID)
    flat_b = weights_b.reshape(rows_b, MID)
    wa = lax.all_gather(flat_a.astype(BF16), ("gx", "gy"), axis=0, tiled=True)
    wb = lax.all_gather(flat_b.astype(BF16), ("gx", "gy"), axis=0, tiled=True)
    out = both_blocks(
        groups,
        images,
        cots,
        wa,
        wb,
        mask,
        jnp.full((1, MID), local_pixels, F32),
        gains_narrow,
        gains_wide,
    )
    image_grads, (dwa, dwb, totals) = out[:3], out[3:]

    def scattered(grads):
        return lax.psum_scatter(grads, ("gx", "gy"), scatter_dimension=0, tiled=True).astype(F32)

    share_a, share_b = scattered(dwa), scattered(dwb)
    device = lax.axis_index(("gx", "gy"))
    masks_a = layer_masks(device * rows_a, rows_a, [ROW_RA, ROW_SA, ROW_EA, ROW_PA, END_A])
    masks_b = layer_masks(device * rows_b, rows_b, [ROW_RB, ROW_SB, ROW_EB, END_B])

    def layer_squares(masks, flat):
        return jnp.sum(masks * jnp.sum(flat * flat, axis=1)[None, :], axis=1)

    weight_squares = jnp.concatenate([layer_squares(masks_a, flat_a), layer_squares(masks_b, flat_b)])
    grad_squares = jnp.concatenate([layer_squares(masks_a, share_a), layer_squares(masks_b, share_b)])
    partial_norms = jnp.stack([weight_squares, grad_squares], axis=1)

    def narrow(e):
        return jnp.stack([totals[e, 1], totals[e, 0]])

    def wide(e, cross):
        return jnp.stack(
            [totals[e, cross : cross + WIDE].reshape(-1), totals[e, :WIDE].reshape(-1)]
        )

    sums_narrow = jnp.stack([narrow(11), narrow(10), narrow(8), narrow(7)])
    sums_wide = jnp.stack([wide(9, WIDE), wide(9, 2 * WIDE), wide(6, WIDE)])
    total_narrow, total_wide = lax.psum((sums_narrow, sums_wide), "gy")
    total_norms, pixels_total = lax.psum((partial_norms, local_pixels), ("gx", "gy"))
    weight_norm = jnp.sqrt(total_norms[:, 0])
    grad_norm = jnp.sqrt(total_norms[:, 1]) / pixels_total
    trust_ratio = TRUST_SCALE * weight_norm / (grad_norm + WEIGHT_DECAY * weight_norm)

    def update(masks, trust, share, flat, moment):
        trust_rows = jnp.sum(masks * trust[:, None], axis=0)[:, None]
        step = LEARN_RATE * trust_rows * (share / pixels_total + WEIGHT_DECAY * flat)
        return MOMENTUM * moment + step.reshape(-1)

    return (
        *image_grads,
        update(masks_a, trust_ratio[:4], share_a, flat_a, moment_a),
        update(masks_b, trust_ratio[4:], share_b, flat_b, moment_b),
        MOMENTUM * gain_moment_narrow + GAIN_RATE * (total_narrow / pixels_total),
        MOMENTUM * gain_moment_wide + GAIN_RATE * (total_wide / pixels_total),
        jnp.stack([weight_norm, grad_norm], axis=1),
    )


def solution(mesh):
    split = P(("gx", "gy"))
    in_specs = (split,) * 11 + (P(),) * 4
    out_specs = (split,) * 5 + (P(),) * 3
    return jax.shard_map(body, mesh=mesh, in_specs=in_specs, out_specs=out_specs, check_vma=False)
```

```python
import functools

import jax
import jax.numpy as jnp
import numpy as np
from jax import lax
from jax.experimental import pallas as pl
from jax.experimental.pallas import tpu as pltpu
from jax.sharding import PartitionSpec as P

C_IN = 1024
MID = 512
C_OUT = 2048

EPSILON = 1e-05
MOMENTUM = 0.9
LEARN_RATE = 20.0
TRUST_SCALE = 0.001
WEIGHT_DECAY = 5e-05
GAIN_RATE = 0.2

MESH = pl.DeviceIdType.MESH
F32 = jnp.float32
BF16 = jnp.bfloat16
TILE = 256
ROWS = 64
WIDE = C_OUT // MID
LANE_ROWS = MID // 128

ROW_RA, ROW_SA, ROW_EA, ROW_PA = 0, C_IN, C_IN + 9 * MID, C_IN + 9 * MID + C_OUT
END_A = ROW_PA + C_IN * WIDE
ROW_RB, ROW_SB, ROW_EB = 0, C_OUT, C_OUT + 9 * MID
END_B = ROW_EB + C_OUT

EXCHANGES = 12
FIRST = [8 * e + 8 * sum(wide < e for wide in (2, 9)) for e in range(EXCHANGES)]
SUM_ROWS = 8 * (EXCHANGES + 2)


GATHER_STEPS = (
    (("near", 0, 0),),
    (("far", 0, 0), ("near", 1, 0), ("own", 0, 1)),
    (("far", 1, 0), ("near", 0, 1), ("own", 0, 2)),
    (("far", 0, 1), ("near", 0, 2), ("own", 0, 3)),
    (("far", 0, 2),),
    (("own", 1, 1), ("near", 0, 3)),
    (),
    (),
    (),
    (("far", 0, 3), ("own", 1, 2), ("own", 1, 3), ("near", 1, 1)),
    (),
    (("far", 1, 1), ("near", 1, 2)),
    (("near", 1, 3), ("far", 1, 2)),
    (),
    (("far", 1, 3),),
)


def round_up(value, unit):
    return -(-value // unit) * unit


class Layout:
    def __init__(self, shapes):
        pictures = [
            (shape[1] // 2, res, slot)
            for res, shape in enumerate(shapes)
            for slot in range(shape[0])
        ]
        self.sizes = [(shape[1] // 2, shape[0]) for shape in shapes]
        pictures.sort(key=lambda item: (-item[0], item[2]))
        self.tiles = []
        self.fill = []
        for side, res, slot in pictures:
            for tile in range(len(self.tiles) + 1):
                if tile == len(self.tiles):
                    self.tiles.append([])
                    self.fill.append(0)
                if self.fill[tile] + side * side <= TILE:
                    self.tiles[tile].append((side, res, slot, self.fill[tile]))
                    self.fill[tile] += side * side
                    break
        self.rows = TILE * len(self.tiles)

    def row_codes(self):
        codes = np.full((self.rows, 1), -1, np.int32)
        for tile, members in enumerate(self.tiles):
            for side, res, slot, start in members:
                first = tile * TILE + start
                codes[first : first + side * side] = (res << 16) + slot
        return codes

    def neighbours(self):
        table = np.full((16, self.rows), -1, np.int32)
        for tap in range(9):
            down, right = tap // 3 - 1, tap % 3 - 1
            for tile, members in enumerate(self.tiles):
                for side, _, _, start in members:
                    for i in range(side):
                        for j in range(side):
                            if 0 <= i + down < side and 0 <= j + right < side:
                                table[tap, tile * TILE + start + i * side + j] = (
                                    start + (i + down) * side + j + right
                                )
        return table

    def picture_rows(self, step):
        result = []
        for members in self.tiles:
            for res, (side, slots) in enumerate(self.sizes):
                codes = np.full((step, side, side * step, slots), -1, np.int32)
                for member_side, member_res, slot, start in members:
                    if member_res == res:
                        for i in range(side):
                            for c in range(side * step):
                                for p in range(step):
                                    row = start + i * side + c // step
                                    codes[p, i, c, slot] = (2 * p + c % step) * TILE + row
                result += [codes[p].reshape(-1) for p in range(step)]
        return result

    def picture_back(self):
        result = []
        for res, (side, slots) in enumerate(self.sizes):
            for p in range(2):
                back = np.full((2, self.rows), -1, np.int32)
                for tile, members in enumerate(self.tiles):
                    for member_side, member_res, slot, start in members:
                        if member_res == res:
                            for i in range(side):
                                for c in range(2 * side):
                                    row = tile * TILE + start + i * side + c // 2
                                    back[c % 2, row] = (i * 2 * side + c) * slots + slot
                result += [back.reshape(-1)]
        return np.stack(result)

    def tiles_of(self, res):
        return [tile for tile, members in enumerate(self.tiles) if any(m[1] == res for m in members)]


def dot(left, right):
    return jnp.dot(left, right, preferred_element_type=F32)


def dot_tn(left, right):
    return lax.dot_general(left, right, (((0,), (0,)), ((), ())), preferred_element_type=F32)


def dot_nt(left, right):
    return lax.dot_general(left, right, (((1,), (1,)), ((), ())), preferred_element_type=F32)


def sigmoid(value):
    return 0.5 * jnp.tanh(0.5 * value) + 0.5


def one_hot(targets, count, offset=0):
    ids = lax.broadcasted_iota(jnp.int32, (count, targets.shape[1]), 0) + offset
    return jnp.where(ids == targets, 1.0, 0.0).astype(BF16)


def loop(count, body, unroll=1):
    def step(index, carry):
        body(index)
        return carry

    lax.fori_loop(0, count, step, 0, unroll=unroll)


def columns(index, width=MID):
    if isinstance(index, int):
        return pl.ds(index * width, width)
    return pl.ds(pl.multiple_of(index * width, width), width)


INPUTS = [
    "img_s",
    "img_m",
    "img_l",
    "cot_s",
    "cot_m",
    "cot_l",
    "wa",
    "wb",
    "gains_n",
    "gains_w",
    "shifts",
    "codes_img",
    "codes_cot",
    "codes_back",
    "codes_row",
    "counts_in",
]
DIRECT_INPUTS = [
    "moment_a",
    "moment_b",
    "gain_moment_n",
    "gain_moment_w",
]
SCRATCH = [
    "z_one",
    "z_main",
    "z_side",
    "z_six",
    "g_wide",
    "middle",
    "cot_p",
    "gp_side",
    "act_one",
    "z_two",
    "z_four",
    "z_five",
    "g_nar",
    "act_two",
    "act_four",
    "act_five",
    "gp_nar",
    "shifted",
    "x_p",
    "w_ra",
    "w_sp",
    "w_ea",
    "w_pa",
    "w_rb",
    "w_eb",
    "d_acc",
    "d_out",
    "stats",
    "arrived",
    "par",
    "mask",
    "wsem",
    "rsem",
    "dsem",
    "isem",
    "xsend",
    "xrecv",
]
OUTPUTS = [
    "out_s",
    "out_m",
    "out_l",
    "dwa",
    "dwb",
    "totals",
]
DIRECT_OUTPUTS = [
    "new_a",
    "new_b",
    "new_gain_n",
    "new_gain_w",
    "norms_out",
    "all_a",
    "all_b",
    "r1_a",
    "r1_b",
    "r2_a",
    "r2_b",
    "r3_a",
    "r3_b",
    "r4_a",
    "r4_b",
]
DIRECT_SCRATCH = [
    "in_one",
    "in_two",
    "in_three",
    "part_b",
    "flat",
    "gain_sums",
    "gain_got",
    "norms",
    "norm_got",
    "norm_all",
    "lsem",
    "gsend",
    "grecv",
    "fsend",
    "frecv",
    "ssend",
    "srecv",
    "hsem",
    "asend",
    "arecv",
    "bsend",
    "brecv",
    "csend",
    "crecv",
]


class Named:
    def __init__(self, names, refs):
        self.__dict__.update(zip(names, refs, strict=True))


def mega(names, layout, groups, direct, *refs):
    r = Named(names, refs)
    img_s = r.img_s
    img_m = r.img_m
    img_l = r.img_l
    cot_s = r.cot_s
    cot_m = r.cot_m
    cot_l = r.cot_l
    wa = r.wa
    wb = r.wb
    codes_row = r.codes_row
    counts_in = r.counts_in
    mask = r.mask
    gains_n = r.gains_n
    gains_w = r.gains_w
    shifts = r.shifts
    codes_img = r.codes_img
    codes_cot = r.codes_cot
    codes_back = r.codes_back
    out_s = r.out_s
    out_m = r.out_m
    out_l = r.out_l
    dwa = r.dwa
    dwb = r.dwb
    totals = r.totals
    z_one = r.z_one
    z_main = r.z_main
    z_side = r.z_side
    z_six = r.z_six
    g_wide = r.g_wide
    middle = r.middle
    cot_p = r.cot_p
    gp_side = r.gp_side
    act_one = r.act_one
    z_two = r.z_two
    z_four = r.z_four
    z_five = r.z_five
    g_nar = r.g_nar
    act_two = r.act_two
    act_four = r.act_four
    act_five = r.act_five
    gp_nar = r.gp_nar
    shifted = r.shifted
    x_p = r.x_p
    w_ra = r.w_ra
    w_sp = r.w_sp
    w_ea = r.w_ea
    w_pa = r.w_pa
    w_rb = r.w_rb
    w_eb = r.w_eb
    d_acc = r.d_acc
    d_out = r.d_out
    stats = r.stats
    arrived = r.arrived
    par = r.par
    wsem = r.wsem
    rsem = r.rsem
    dsem = r.dsem
    isem = r.isem
    xsend = r.xsend
    xrecv = r.xrecv
    rows = layout.rows
    tiles = len(layout.tiles)
    steps = rows // ROWS
    me_x = lax.axis_index("gx")
    me_y = lax.axis_index("gy")

    y, x, core = me_y // 4, (me_y // 2) % 2, me_y % 2
    to_x = (y * 2 + 1 - x) * 2 + core
    to_y = ((1 - y) * 2 + x) * 2 + core
    across = ((1 - y) * 2 + 1 - x) * 2 + core
    twin = (y * 2 + x) * 2 + 1 - core

    barrier = pltpu.get_barrier_semaphore()
    greeted = [(lax.rem(me_x + hop, groups), me_y) for hop in range(1, groups)]
    if direct:
        greeted += [(me_x, lax.rem(me_y + hop, 8)) for hop in range(1, 8)]
    for device in greeted:
        pl.semaphore_signal(barrier, inc=1, device_id=device, device_id_type=MESH)

    if direct:
        counts = (wa.shape[0] // LANE_ROWS, wb.shape[0] // LANE_ROWS)
        shards = (r.in_three, r.in_two.at[pl.ds(0, counts[1])])
    else:
        counts = (wa.shape[0], wb.shape[0])
    halves = (counts[0] - counts[0] // 32 * 16, counts[1] // 32 * 16)
    if direct:
        full_a, full_b = r.all_a, r.all_b
    else:
        full_a, full_b = wa, wb
    alls = (full_a, full_b)

    def span(first, count):
        return pl.ds(first if isinstance(first, int) else pl.multiple_of(first, 16), count)

    def part_of(i, which):
        count, cut = counts[i], halves[i]
        return {"low": (0, cut), "high": (cut, count - cut), "all": (0, count)}[which]

    def remote(source, target, send_sem, recv_sem, device):
        return pltpu.make_async_remote_copy(
            src_ref=source,
            dst_ref=target,
            send_sem=send_sem,
            recv_sem=recv_sem,
            device_id=device,
            device_id_type=MESH,
        )

    def along_z(i, hop):
        here = alls[i].at[span((me_x * 8 + me_y) * counts[i], counts[i])]
        device = (lax.rem(me_x + hop, groups), me_y)
        return remote(shards[i], here, r.fsend.at[i, hop - 1], r.frecv.at[i, me_x], device)

    def from_z(i, zz):
        here = alls[i].at[span((zz * 8 + me_y) * counts[i], counts[i])]
        return remote(shards[i], here, r.fsend.at[i, 0], r.frecv.at[i, zz], (me_x, me_y))

    spread_plan = (
        (me_y, "all", to_x),
        (me_y, "all", to_y),
        (me_y, "all", twin),
        (to_x, "low", to_y),
        (to_x, "all", twin),
        (to_y, "high", to_x),
        (to_y, "all", twin),
        (across, "low", twin),
        (across, "high", twin),
    )

    def spread(i, zz, k):
        owner, which, target = spread_plan[k]
        low, count = part_of(i, which)
        here = alls[i].at[span((zz * 8 + owner) * counts[i] + low, count)]
        unit = i * 4 + zz
        return remote(here, here, r.gsend.at[unit, k], r.grecv.at[unit, k], (me_x, target))

    def spread_own(i, zz):
        @pl.when(zz != me_x)
        def _():
            from_z(i, zz).wait_recv()

        for k in (0, 1, 2):
            spread(i, zz, k).start()

    def spread_near(i, zz):
        for got, onward in ((0, (3, 4)), (1, (5, 6))):
            spread(i, zz, got).wait_recv()
            for k in onward:
                spread(i, zz, k).start()

    def spread_far(i, zz):
        for got, onward in ((3, 7), (5, 8)):
            spread(i, zz, got).wait_recv()
            spread(i, zz, onward).start()

    def spread_done(i, zz):
        for k in (2, 4, 6, 7, 8):
            spread(i, zz, k).wait_recv()

    def turn(k):
        return me_x if k == 0 else k - 1 + (k + 3 - me_x) // 4

    def own(i, k):
        if direct:
            spread_own(i, turn(k))

    def pass_on(place):
        if direct:
            for step in GATHER_STEPS[place]:
                {"own": spread_own, "near": spread_near, "far": spread_far}[step[0]](step[1], turn(step[2]))

    def done(i, zz):
        if direct:
            spread_done(i, zz)

    def fetch(source, first, count, target, sem):
        return pltpu.make_async_copy(source.at[pl.ds(first, count)], target, wsem.at[sem])

    cut = min(max(8 * counts[0] - ROW_SA, 0), 9 * MID) if direct else 4 * MID
    get_ra = fetch(full_a, ROW_RA, C_IN, w_ra, 0)
    get_sa_low = fetch(full_a, ROW_SA, cut, w_sp.at[pl.ds(0, cut)], 1)
    get_sa_high = fetch(full_a, ROW_SA + cut, 9 * MID - cut, w_sp.at[pl.ds(cut, 9 * MID - cut)], 4)
    get_sa = fetch(full_a, ROW_SA, 9 * MID, w_sp, 1)
    get_rb = fetch(full_b, ROW_RB, C_OUT, w_rb, 2)
    get_sb = fetch(full_b, ROW_SB, 9 * MID, w_sp, 3)

    dws = (dwa, dwb)
    if direct:
        r_one, r_two, r_three = (r.r1_a, r.r1_b), (r.r2_a, r.r2_b), (r.r3_a, r.r3_b)
        r_four, parts = (r.r4_a, r.r4_b), (w_rb, r.part_b)
    work = (z_six, w_eb, middle)

    def piece(i, zz, slot, which_one):
        count, unit = counts[i], i * 4 + zz
        low, low_count = part_of(i, "low")
        high, high_count = part_of(i, "high")
        at = work[slot].at
        plan = []
        for q in range(4):
            source = dws[i].at[span((zz * 8 + q * 2 + 1 - core) * count, count)]
            plan.append((source, r_one[i].at[span((zz * 4 + q) * count, count)], twin))
        for k in range(2):
            source = at[span((k * 2 + 1 - x) * count + low, low_count)]
            plan.append((source, r_two[i].at[span((zz * 2 + k) * count + low, low_count)], to_x))
        for k in range(2):
            source = at[span(((1 - y) * 2 + k) * count + high, high_count)]
            plan.append((source, r_two[i].at[span((zz * 2 + k) * count + high, high_count)], to_y))
        source = at[span(((1 - y) * 2 + x) * count + low, low_count)]
        plan.append((source, r_three[i].at[span(zz * count + low, low_count)], to_y))
        source = at[span((y * 2 + 1 - x) * count + high, high_count)]
        plan.append((source, r_three[i].at[span(zz * count + high, high_count)], to_x))
        source, target, device = plan[which_one]
        sems = r.ssend.at[unit, which_one], r.srecv.at[unit, which_one]
        return remote(source, target, *sems, (me_x, device))

    def local(source, target, sem):
        return pltpu.make_async_copy(source, target, r.lsem.at[sem])

    def loads_one(i, zz, slot):
        count = counts[i]
        result = [
            local(
                dws[i].at[span((zz * 8 + q * 2 + core) * count, count)],
                work[slot].at[span(q * count, count)],
                q,
            )
            for q in range(4)
        ]
        arrivals = r_one[i].at[span(zz * 4 * count, 4 * count)]
        return result + [local(arrivals, r.in_one.at[span(0, 4 * count)], 4)]

    def load_two(i, zz):
        count = 2 * counts[i]
        return local(r_two[i].at[span(zz * count, count)], r.in_two.at[span(0, count)], 5)

    def load_three(i, zz):
        count = counts[i]
        return local(r_three[i].at[span(zz * count, count)], r.in_three.at[span(0, count)], 6)

    def add_rows(target, target_first, left, left_first, right, right_first, count):
        step = 32 if count % 32 == 0 else 16

        def body(index):
            def at(first):
                return span(first + index * step, step)

            total = left[at(left_first), :].astype(F32) + right[at(right_first), :].astype(F32)
            target[at(target_first), :] = total.astype(BF16)

        loop(count // step, body, unroll=2)

    def sum_send(i, zz, slot):
        for k in range(4):
            piece(i, zz, slot, k).start()

    def sum_one_load(i, zz, slot, before):
        if before is not None:
            for k in range(4, 10):
                piece(before[0], before[1], slot, k).wait_send()
        for k in range(4):
            piece(i, zz, slot, k).wait_recv()
        for copy in loads_one(i, zz, slot):
            copy.start()

    def sum_one(i, zz, slot):
        for copy in loads_one(i, zz, slot):
            copy.wait()
        add_rows(work[slot], 0, work[slot], 0, r.in_one, 0, 4 * counts[i])
        for k in range(4, 8):
            piece(i, zz, slot, k).start()

    def sum_two_load(i, zz, slot):
        for k in range(4, 8):
            piece(i, zz, slot, k).wait_recv()
        load_two(i, zz).start()

    def sum_two(i, zz, slot):
        load_two(i, zz).wait()
        count = counts[i]
        low, low_count = part_of(i, "low")
        high, high_count = part_of(i, "high")
        for k in range(2):
            first = (k * 2 + x) * count + low
            add_rows(work[slot], first, work[slot], first, r.in_two, k * count + low, low_count)
            first = (y * 2 + k) * count + high
            add_rows(work[slot], first, work[slot], first, r.in_two, k * count + high, high_count)
        for k in range(8, 10):
            piece(i, zz, slot, k).start()

    def sum_three_load(i, zz, slot):
        for k in range(8, 10):
            piece(i, zz, slot, k).wait_recv()
        load_three(i, zz).start()

    def to_z(i, zz):
        count = counts[i]
        return remote(
            parts[i].at[span(zz * count, count)],
            r_four[i].at[span(me_x * count, count)],
            r.ssend.at[i * 4 + zz, 10],
            r.srecv.at[i * 4 + me_x, 10],
            (zz, me_y),
        )

    def sum_three(i, zz, slot):
        load_three(i, zz).wait()
        count = counts[i]
        mine = (y * 2 + x) * count
        add_rows(parts[i], zz * count, work[slot], mine, r.in_three, 0, count)

        @pl.when(zz != me_x)
        def _():
            to_z(i, zz).start()

    def last_sum(i, share):
        count = counts[i]

        def arrived_from(zz):
            here = span(zz * count, count)
            return remote(
                parts[i].at[here], r_four[i].at[here], r.ssend.at[i * 4, 10], r.srecv.at[i * 4 + zz, 10], (me_x, me_y)
            )

        def load(zz):
            here = span(zz * count, count)
            return local(r_four[i].at[here], r.in_one.at[here], zz)

        for zz in range(groups):

            @pl.when(zz != me_x)
            def _():
                arrived_from(zz).wait_recv()
                load(zz).start()

        for zz in range(groups):

            @pl.when(zz != me_x)
            def _():
                load(zz).wait()

            @pl.when(zz == me_x)
            def _():
                r.in_one[span(zz * count, count), :] = parts[i][span(zz * count, count), :]

        total = r.in_one[0:count, :].astype(F32)
        for zz in range(1, groups):
            total = total + r.in_one[zz * count : (zz + 1) * count, :].astype(F32)
        put_flat(total, share, count)

    device = me_x * 8 + me_y
    flat_rows = tuple(LANE_ROWS * count for count in counts)
    layer_bounds = tuple(
        tuple(row * LANE_ROWS for row in bounds)
        for bounds in ((ROW_RA, ROW_SA, ROW_EA, ROW_PA, END_A), (ROW_RB, ROW_SB, ROW_EB, END_B))
    )
    layers_before = (0, len(layer_bounds[0]) - 1)
    share_at = (0, flat_rows[0])
    weight_at = ((d_acc, flat_rows[0] + flat_rows[1] + 32), (r.flat, 0)) if direct else None
    moment_at = (flat_rows[1], flat_rows[1] + flat_rows[0])
    FLAT_STEP = 64

    def put_flat(value, first, count):
        for lane in range(LANE_ROWS):
            part = value[:, lane * 128 : (lane + 1) * 128]
            d_acc[pl.ds(first + lane, count, stride=LANE_ROWS), :] = part

    def in_layer(i, step, layer):
        ids = lax.broadcasted_iota(jnp.int32, (FLAT_STEP, 128), 0) + (device * flat_rows[i] + step * FLAT_STEP)
        return (ids >= layer_bounds[i][layer]) & (ids < layer_bounds[i][layer + 1])

    def layer_squares(i, ref, first, norm_row):
        layers = len(layer_bounds[i]) - 1

        def step(index, sums):
            value = ref[pl.ds(pl.multiple_of(first + index * FLAT_STEP, 32), FLAT_STEP), :]
            square = value * value
            return tuple(
                kept
                + jnp.sum(
                    jnp.where(in_layer(i, index, layer), square, 0.0).reshape(FLAT_STEP // 8, 8, 128), axis=0
                )
                for layer, kept in enumerate(sums)
            )

        start = tuple(jnp.zeros((8, 128), F32) for _ in range(layers))
        sums = lax.fori_loop(0, flat_rows[i] // FLAT_STEP, step, start)
        for layer, value in enumerate(sums):
            row = norm_row + layers_before[i] + layer
            r.norms[row : row + 1, :] = jnp.sum(value, axis=0, keepdims=True)

    def swap_all(axis_size, source, target, slot, device_of, send_sems, recv_sems):
        return [
            remote(source, target.at[slot], send_sems.at[hop - 1], recv_sems.at[hop - 1], device_of(hop))
            for hop in range(1, axis_size)
        ]

    def gain_swap():
        return swap_all(
            8, r.gain_sums, r.gain_got, me_y, lambda hop: (me_x, lax.rem(me_y + hop, 8)), r.asend, r.arecv
        )

    def norm_swap_x():
        return swap_all(
            groups,
            r.norms,
            r.norm_got,
            me_x,
            lambda hop: (lax.rem(me_x + hop, groups), me_y),
            r.bsend,
            r.brecv,
        )

    def norm_swap_y():
        return swap_all(
            8, r.norms, r.norm_all, me_y, lambda hop: (me_x, lax.rem(me_y + hop, 8)), r.csend, r.crecv
        )

    def start_gains():
        rows_of = []
        for e in (11, 10, 8, 7):
            rows_of += [(e, 1), (e, 0)]
        for e, cross in ((9, WIDE), (9, 2 * WIDE), (6, WIDE)):
            rows_of += [(e, cross + j) for j in range(WIDE)] + [(e, j) for j in range(WIDE)]
        for row, (e, source) in enumerate(rows_of):
            r.gain_sums[row : row + 1, :] = totals[e, source : source + 1, :]
        for copy in gain_swap():
            copy.start()
        r.gain_got[pl.ds(me_y, 1)] = r.gain_sums[...][None]

    def flat_loads():
        return [
            pltpu.make_async_copy(wa, d_acc.at[pl.ds(weight_at[0][1], flat_rows[0])], r.hsem.at[0]),
            pltpu.make_async_copy(wb, r.flat.at[pl.ds(0, flat_rows[1])], r.hsem.at[1]),
            pltpu.make_async_copy(r.moment_a, r.flat.at[pl.ds(moment_at[0], flat_rows[0])], r.hsem.at[2]),
            pltpu.make_async_copy(r.moment_b, r.flat.at[pl.ds(moment_at[1], flat_rows[1])], r.hsem.at[3]),
        ]

    def update():
        for copy in norm_swap_x():
            copy.start()
        r.norm_got[pl.ds(me_x, 1)] = r.norms[...][None]
        for copy in norm_swap_x():
            copy.wait()
        total = r.norm_got[0]
        for other in range(1, groups):
            total = total + r.norm_got[other]
        r.norms[...] = total
        for copy in norm_swap_y():
            copy.start()
        r.norm_all[pl.ds(me_y, 1)] = total[None]
        for copy in norm_swap_y():
            copy.wait()
        total = r.norm_all[0]
        for other in range(1, 8):
            total = total + r.norm_all[other]
        over = 1.0 / total[15:16, 0:1]
        lanes = jnp.sum(total, axis=1, keepdims=True)
        weight_norm = jnp.sqrt(lanes[0:7])
        grad_norm = jnp.sqrt(lanes[8:15]) * over
        trust = TRUST_SCALE * weight_norm / (grad_norm + WEIGHT_DECAY * weight_norm)
        first_column = lax.broadcasted_iota(jnp.int32, (7, 2), 1) == 0
        r.norms_out[...] = jnp.where(first_column, weight_norm, grad_norm)
        for copy in gain_swap():
            copy.wait()
        gains = r.gain_got[0]
        for other in range(1, 8):
            gains = gains + r.gain_got[other]
        gains = GAIN_RATE * over * gains
        for k in range(4):
            r.new_gain_n[k] = MOMENTUM * r.gain_moment_n[k] + gains[2 * k : 2 * k + 2]
        for k in range(3):
            for which in range(2):
                for j in range(WIDE):
                    row = 8 + 8 * k + WIDE * which + j
                    here = slice(j * MID, (j + 1) * MID)
                    old = r.gain_moment_w[k, which : which + 1, here]
                    r.new_gain_w[k, which : which + 1, here] = MOMENTUM * old + gains[row : row + 1]
        for copy in flat_loads():
            copy.wait()
        outgoing = []
        for i, target in enumerate((r.new_a, r.new_b)):
            weight_ref, weight_first = weight_at[i]

            def step(index, i=i, weight_ref=weight_ref, weight_first=weight_first):
                def at(first):
                    return pl.ds(pl.multiple_of(first + index * FLAT_STEP, 32), FLAT_STEP)

                rate = jnp.zeros((FLAT_STEP, 128), F32)
                for layer in range(len(layer_bounds[i]) - 1):
                    row = layers_before[i] + layer
                    rate = jnp.where(in_layer(i, index, layer), trust[row : row + 1], rate)
                decayed = d_acc[at(share_at[i]), :] * over + WEIGHT_DECAY * weight_ref[at(weight_first), :]
                here = at(moment_at[i])
                r.flat[here, :] = MOMENTUM * r.flat[here, :] + LEARN_RATE * rate * decayed

            loop(flat_rows[i] // FLAT_STEP, step)
            source = r.flat.at[pl.ds(moment_at[i], flat_rows[i])]
            outgoing.append(pltpu.make_async_copy(source, target, r.hsem.at[i]))
            outgoing[-1].start()
        for copy in outgoing:
            copy.wait()

    sum_order = [(1, 3), (1, 2), (1, 1), (1, 0), (0, 3), (0, 2), (0, 1), (0, 0)]
    ticks = {}
    for u, (i, zz) in enumerate(sum_order):
        slot = u % len(work)
        before = sum_order[u - len(work)] if u >= len(work) else None
        for at_tick, rank, op in (
            (0, 5, functools.partial(sum_one_load, i, zz, slot, before)),
            (1, 2, functools.partial(sum_one, i, zz, slot)),
            (5, 4, functools.partial(sum_two_load, i, zz, slot)),
            (6, 1, functools.partial(sum_two, i, zz, slot)),
            (8, 3, functools.partial(sum_three_load, i, zz, slot)),
            (9, 0, functools.partial(sum_three, i, zz, slot)),
        ):
            ticks.setdefault(3 * u + at_tick, []).append((rank, u, op))
    pending = [
        [op for _, _, op in sorted(ticks.get(tick, []), key=lambda item: item[:2])]
        for tick in range(max(ticks) + 1)
    ]

    pending = [[]] + pending

    def pump(count=1):
        if direct:
            for _ in range(count):
                if pending:
                    for op in pending.pop(0):
                        op()

    def sums_of(*units):
        if direct:
            for i, zz in units:
                sum_send(i, zz, 0)

    def unravel(source, first, count, target, begin=0, end=None):
        end = count * WIDE // TILE if end is None else end
        part = TILE // WIDE
        depth = 2 * MID // TILE

        def raw(chunk):
            slot = lax.rem(chunk, depth)
            return pltpu.make_async_copy(
                source.at[pl.ds(pl.multiple_of(first + chunk * TILE, TILE), TILE)],
                d_out.at[columns(slot, TILE)],
                rsem.at[slot],
            )

        for chunk in range(begin, min(begin + depth - 1, end)):
            raw(jnp.int32(chunk)).start()
        lane = lax.broadcasted_iota(jnp.int32, (1, TILE), 1)
        order = one_hot(lax.rem(lane, WIDE) * part + lax.div(lane, WIDE), TILE)

        def body(step):
            chunk = step + begin

            @pl.when(chunk + depth - 1 < end)
            def _():
                raw(chunk + depth - 1).start()

            raw(chunk).wait()
            sorted_rows = dot(order, d_out[columns(lax.rem(chunk, depth), TILE), :]).astype(BF16)
            where = pl.ds(pl.multiple_of(chunk * part, part), part)
            for k in range(WIDE):
                values = sorted_rows[k * part : (k + 1) * part]
                if target.shape[1] == MID:
                    target[pl.ds(pl.multiple_of(k * count + chunk * part, part), part), :] = values
                else:
                    target[where, k * MID : (k + 1) * MID] = values

        loop(end - begin, body)

    def gather_pictures(refs, codes, step, width, target, after):
        shapes = [(side, side * step, slots) for side, slots in layout.sizes]
        turns = [(block, p) for block in range(width // MID) for p in range(step)]

        def scoped(*buffers):
            raws, flats = buffers[: len(shapes)], buffers[len(shapes) :]

            def copy_of(turn, res):
                block, p = turns[turn]
                source = refs[res].at[:, p, :, :, pl.ds(block * MID, MID)]
                return pltpu.make_async_copy(source, raws[res], isem.at[res])

            for res in range(len(shapes)):
                copy_of(0, res).start()
            for turn, (block, p) in enumerate(turns):
                for res, shape in enumerate(shapes):
                    copy_of(turn, res).wait()
                    flats[res][...] = raws[res][...].reshape(shape[0] * shape[1] * shape[2], MID)
                    if turn + 1 < len(turns):
                        copy_of(turn + 1, res).start()

                def body(index, block=block, p=p):
                    kind = 2 * p + index
                    for tile in range(tiles):
                        total = None
                        for res, shape in enumerate(shapes):
                            if tile in layout.tiles_of(res):
                                row = (tile * len(shapes) + res) * step + p
                                lanes = codes[row : row + 1, : flats[res].shape[0]]
                                term = dot(one_hot(lanes, TILE, kind * TILE), flats[res][...])
                                total = term if total is None else total + term
                        here = slice(tile * TILE, (tile + 1) * TILE)
                        target[here, columns(kind * (width // MID) + block)] = total.astype(BF16)

                loop(step, body)
                after(turn)

        pl.run_scoped(
            scoped,
            *[pltpu.VMEM((*shape, MID), BF16) for shape in shapes],
            *[pltpu.VMEM((shape[0] * shape[1] * shape[2], MID), BF16) for shape in shapes],
        )

    if direct:
        incoming = [
            pltpu.make_async_copy(source, d_acc.at[pl.ds(share_at[i], flat_rows[i])], r.hsem.at[i])
            for i, source in enumerate((wa, wb))
        ]
        for copy in incoming:
            copy.start()
        for copy in incoming:
            copy.wait()
        for i in range(2):
            for lane in range(LANE_ROWS):
                values = d_acc[pl.ds(share_at[i] + lane, counts[i], stride=LANE_ROWS), :]
                shards[i][:, lane * 128 : (lane + 1) * 128] = values.astype(BF16)
    pl.semaphore_wait(barrier, len(greeted))
    if direct:
        copies_own = [
            pltpu.make_async_copy(
                shards[i], alls[i].at[span((me_x * 8 + me_y) * counts[i], counts[i])], wsem.at[2 * i]
            )
            for i in range(2)
        ]
        for i in range(2):
            copies_own[i].start()
            for hop in range(1, groups):
                along_z(i, hop).start()
            copies_own[i].wait()
            spread_own(i, me_x)
        r.norms[...] = jnp.zeros(r.norms.shape, F32)
        for i in range(2):
            layer_squares(i, d_acc, share_at[i], 0)
    present = [counts_in[0, res] for res in range(3)]
    local_pixels = sum(
        present[res] * side * side for res, side in {(m[1], m[0]) for tile in layout.tiles for m in tile}
    ).astype(F32)
    ids = codes_row[...]
    limits = [(res << 16, (res << 16) + present[res]) for res in range(3)]
    inside = [(ids >= low) & (ids < high) for low, high in limits]
    mask[...] = jnp.where(inside[0] | inside[1] | inside[2], 1.0, 0.0)

    def copies_of(e, count):
        return [
            pltpu.make_async_remote_copy(
                src_ref=stats.at[pl.ds(FIRST[e], count)],
                dst_ref=arrived.at[me_x, pl.ds(FIRST[e], count)],
                send_sem=xsend.at[e, hop - 1],
                recv_sem=xrecv.at[e, hop - 1],
                device_id=(lax.rem(me_x + hop, groups), me_y),
                device_id_type=MESH,
            )
            for hop in range(1, groups)
        ]

    def send(e, count):
        for copy in copies_of(e, count):
            copy.start()
        here = slice(FIRST[e], FIRST[e] + count)
        arrived[pl.ds(me_x, 1), here] = stats[here][None]

    def receive(e, count):
        for copy in copies_of(e, count):
            copy.wait()
        here = slice(FIRST[e], FIRST[e] + count)
        total = arrived[0, here]
        for other in range(1, groups):
            total = total + arrived[other, here]
        totals[e, :count] = total

    def each(width, body):
        def step(index):
            block, step_row = index // steps, lax.rem(index, steps)
            body(pl.ds(pl.multiple_of(step_row * ROWS, ROWS), ROWS), block)

        loop(width * steps, step, unroll=2)

    def each_sums(width, body, e, targets):
        def block_step(block):
            def step(index, carry):
                values = body(pl.ds(pl.multiple_of(index * ROWS, ROWS), ROWS), block)
                return tuple(
                    kept + jnp.sum(value.reshape(ROWS // 8, 8, MID), axis=0)
                    for kept, value in zip(carry, values)
                )

            start = tuple(jnp.zeros((8, MID), F32) for _ in targets(0))
            sums = lax.fori_loop(0, steps, step, start, unroll=2)
            for row, value in zip(targets(block), sums):
                stats[pl.ds(FIRST[e] + row, 1)] += jnp.sum(value, axis=0, keepdims=True)

        loop(width, block_step)

    def moments(source, e, width, same=False, first=0):
        def body(here, block):
            value = source[here, columns(block)].astype(F32)
            kept = value * mask[here, :]
            return kept, kept * value

        if same:
            each_sums(width, body, e, lambda block: (first, first + 1))
        else:
            each_sums(width, body, e, lambda block: (first + block, first + width + block))

    def pixel_row():
        return totals[0, 2:3]

    def coefficients(e, first, width, gain_rows, k, pixel_scale):
        count = pixel_row() * pixel_scale
        for j in range(width):
            center = totals[e, first + j : first + j + 1] / count
            square = totals[e, first + width + j : first + width + j + 1] / count
            factor = lax.rsqrt(square - center * center + EPSILON)
            gain, offset = gain_rows(j)
            scale = gain * factor
            par[k, j : j + 1] = scale
            par[k, width + j : width + j + 1] = offset - center * scale
            par[k, 2 * width + j : 2 * width + j + 1] = factor
            par[k, 3 * width + j : 3 * width + j + 1] = -center * factor

    def narrow_gains(k):
        return lambda j: (gains_n[k, 0:1, :], gains_n[k, 1:2, :])

    def wide_gains(k):
        return lambda j: (
            gains_w[k, 0:1, j * MID : (j + 1) * MID],
            gains_w[k, 1:2, j * MID : (j + 1) * MID],
        )

    def row_of(k, which, width, block):
        return par[k, pl.ds(which * width + block, 1)]

    def back_coefficients(e, sum_first, cross_first, width, k, pixel_scale):
        count = pixel_row() * pixel_scale
        for j in range(width):
            total_g = totals[e, sum_first + j : sum_first + j + 1]
            total_x = totals[e, cross_first + j : cross_first + j + 1]
            scale = par[k, j : j + 1]
            factor = par[k, 2 * width + j : 2 * width + j + 1]
            shift = par[k, 3 * width + j : 3 * width + j + 1]
            par[k + 8, j : j + 1] = scale * (total_g + shift * total_x) / count
            par[k + 8, width + j : width + j + 1] = scale * factor * total_x / count

    def activate(source, target, k):
        def body(here, block):
            value = source[here, columns(block)].astype(F32)
            value = value * row_of(k, 0, 1, 0) + row_of(k, 1, 1, 0)
            target[here, columns(block)] = (value * sigmoid(value)).astype(BF16)

        each(source.shape[1] // MID, body)

    def slope(value):
        s = sigmoid(value)
        return s * (1.0 + value * (1.0 - s))

    def back_activate(grad, source, k, e, same=False):
        def body(here, block):
            z = source[here, columns(block)].astype(F32)
            g = grad[here, columns(block)] * slope(z * row_of(k, 0, 1, 0) + row_of(k, 1, 1, 0))
            grad[here, columns(block)] = g
            return g, g * (z * row_of(k, 2, 1, 0) + row_of(k, 3, 1, 0))

        each_sums(source.shape[1] // MID, body, e, lambda block: (0, 1))

    def back_norm(grad, source, target, k, width, same=False):
        def body(here, block):
            j = 0 if same else block
            z = source(here, block) if callable(source) else source[here, columns(block)].astype(F32)
            g = grad[here, columns(block)]
            fixed = row_of(k + 8, 0, width, j) + z * row_of(k + 8, 1, width, j)
            value = g * row_of(k, 0, width, j) - mask[here, :] * fixed
            target[here, columns(block)] = value.astype(BF16)

        each(target.shape[1] // MID, body)

    def shift_into(source, block, table_row, target):
        for tile in range(tiles):
            here = slice(tile * TILE, (tile + 1) * TILE)
            pick = one_hot(shifts[pl.ds(table_row, 1), here], TILE)
            target[here, :] = dot(pick, source[here, columns(block)]).astype(BF16)

    def strided_tap(tap):
        p, q = tap // 3, lax.rem(tap, 3)
        kind = 2 * lax.rem(p + 1, 2) + lax.rem(q + 1, 2)
        return kind, ((p + 1) // 2) * 3 + (q + 1) // 2

    def tap_weight(tap):
        return w_sp[columns(tap), :]

    stats[...] = jnp.zeros(stats.shape, F32)

    image_places = {1: 0, 3: 1}
    gather_pictures(
        (img_s, img_m, img_l),
        codes_img,
        2,
        C_IN,
        x_p,
        lambda turn: pass_on(image_places[turn]) if turn in image_places else None,
    )
    cot_places = {1: 2, 3: 3}
    gather_pictures(
        (cot_s, cot_m, cot_l),
        codes_cot,
        1,
        C_OUT,
        cot_p,
        lambda turn: pass_on(cot_places[turn]) if turn in cot_places else None,
    )
    done(0, 0)
    get_ra.start()
    get_sa_low.start()
    get_ra.wait()

    def first_product(kind):
        z_one[:, columns(kind)] = dot(x_p[:, columns(kind, C_IN)], w_ra[...]).astype(z_one.dtype)

    loop(4, first_product)
    moments(z_one, 0, 4, same=True)
    stats[2:3] = jnp.full((1, MID), local_pixels, F32)
    send(0, 8)
    pass_on(4)
    done(0, 1)
    get_sa_high.start()
    receive(0, 8)
    coefficients(0, 0, 1, narrow_gains(0), 0, 4.0)
    activate(z_one, act_one, 0)

    pass_on(5)
    get_sa_low.wait()
    get_sa_high.wait()
    z_two[...] = jnp.zeros(z_two.shape, F32)

    def conv_a(tap):
        kind, table_row = strided_tap(tap)
        shift_into(act_one, kind, 8 - table_row, shifted)
        z_two[...] += dot(shifted[...], tap_weight(tap))

    for start in range(0, 9, 3):
        loop(3, lambda step, start=start: conv_a(start + step), 3)
        pass_on(6 + start // 3)
    moments(z_two, 1, 1)
    send(1, 8)
    pass_on(9)
    done(0, 2)
    unravel(full_a, ROW_EA, MID, w_ea)
    ready = max(8 * 3 * counts[0] - ROW_PA, 0) // TILE if direct else 0
    if ready:
        unravel(full_a, ROW_PA, C_IN, w_pa, 0, ready)
    pass_on(10)
    done(0, 3)
    unravel(full_a, ROW_PA, C_IN, w_pa, ready)

    def side_product(block):
        z_side[:, columns(block)] = dot(x_p[:, :C_IN], w_pa[:, columns(block)]).astype(z_side.dtype)

    loop(WIDE, side_product)
    pass_on(11)
    moments(z_side, 2, WIDE, first=8)
    receive(1, 8)
    coefficients(1, 0, 1, narrow_gains(1), 1, 1.0)
    activate(z_two, act_two, 1)

    def main_product(block):
        z_main[:, columns(block)] = dot(act_two[...], w_ea[:, columns(block)]).astype(z_main.dtype)

    loop(WIDE, main_product)
    moments(z_main, 2, WIDE)
    pass_on(12)
    send(2, 16)
    pass_on(13)
    done(1, 0)
    get_rb.start()
    receive(2, 16)
    coefficients(2, 0, WIDE, wide_gains(0), 4, 1.0)
    coefficients(2, 8, WIDE, wide_gains(1), 5, 1.0)

    def joined_a(here, block):
        main = z_main[here, columns(block)].astype(F32)
        side = z_side[here, columns(block)].astype(F32)
        value = main * row_of(4, 0, WIDE, block) + row_of(4, 1, WIDE, block)
        return main, side, value + side * row_of(5, 0, WIDE, block) + row_of(5, 1, WIDE, block)

    def block_rows(here, block):
        return pl.ds(pl.multiple_of(block * rows + here.start, ROWS), ROWS)

    def middle_step(here, block):
        _, _, value = joined_a(here, block)
        middle[block_rows(here, block), :] = (value * sigmoid(value)).astype(BF16)

    each(WIDE, middle_step)
    pass_on(14)
    get_rb.wait()
    four = dot(middle[columns(0), :], w_rb[columns(0), :])
    for block in range(1, WIDE):
        four = four + dot(middle[columns(block), :], w_rb[columns(block), :])
    z_four[...] = four
    moments(z_four, 3, 1)
    send(3, 8)
    for zz in range(1, 4):
        done(1, zz)
    get_sb.start()
    unravel(full_b, ROW_EB, MID, w_eb)
    receive(3, 8)
    coefficients(3, 0, 1, narrow_gains(2), 2, 1.0)
    activate(z_four, act_four, 2)

    get_sb.wait()
    z_five[...] = jnp.zeros(z_five.shape, F32)

    def conv_b(tap):
        shift_into(act_four, 0, 8 - tap, shifted)
        z_five[...] += dot(shifted[...], tap_weight(tap))

    loop(9, conv_b, 3)
    moments(z_five, 4, 1)
    send(4, 8)
    receive(4, 8)
    coefficients(4, 0, 1, narrow_gains(3), 3, 1.0)
    activate(z_five, act_five, 3)

    def last_product(block):
        z_six[columns(block), :] = dot(act_five[...], w_eb[columns(block), :]).astype(z_six.dtype)

    loop(WIDE, last_product)
    def six(here, block):
        return z_six[block_rows(here, block), :].astype(F32)

    def last_moments(here, block):
        value = six(here, block)
        kept = value * mask[here, :]
        return kept, kept * value

    each_sums(WIDE, last_moments, 5, lambda block: (block, WIDE + block))
    send(5, 8)
    receive(5, 8)
    coefficients(5, 0, WIDE, wide_gains(2), 6, 1.0)

    if direct:
        for i in range(2):
            for hop in range(1, groups):
                along_z(i, hop).wait_send()

    def turn_over(array, row=0, block=0):
        here = (pl.ds(row, MID), columns(block))
        array[here] = array[here].T

    def output_step(here, block):
        z = six(here, block)
        value = z * row_of(6, 0, WIDE, block) + row_of(6, 1, WIDE, block)
        value = value + middle[block_rows(here, block), :].astype(F32)
        g = cot_p[here, columns(block)].astype(F32) * mask[here, :] * slope(value)
        g_wide[here, columns(block)] = g
        return g, g * (z * row_of(6, 2, WIDE, block) + row_of(6, 3, WIDE, block))

    each_sums(WIDE, output_step, 6, lambda block: (block, WIDE + block))
    send(6, 8)
    turn_over(act_five)
    turn_over(act_four)
    turn_over(act_two)
    receive(6, 8)
    back_coefficients(6, 0, WIDE, WIDE, 6, 1.0)
    gp_six = cot_p
    back_norm(g_wide, six, gp_six, 6, WIDE)

    def put(unit, first, target, slot):
        return pltpu.make_async_copy(
            d_out.at[columns(slot)],
            target.at[pl.ds(pl.multiple_of(first + unit * MID, MID), MID)],
            dsem.at[slot],
        )

    def store_unit(step, first, target, value, unit=None):
        slot = lax.rem(step, 2) if not isinstance(step, int) else step % 2
        unit = step if unit is None else unit

        @pl.when(step >= 2)
        def _():
            put(unit, first, target, slot).wait()

        d_out[columns(slot), :] = value.astype(BF16)
        put(unit, first, target, slot).start()

    def flush_one(slot, first, target):
        put(0, first, target, slot).wait()

    def flush(first, target):
        for slot in range(2):
            flush_one(slot, first, target)

    def wide_weight_grad(left, left_count, grad, first, target):
        def body(chunk):
            part = left(chunk)
            for k in range(WIDE):
                value = dot(part, grad[:, columns(k)])
                for lane in range(LANE_ROWS):
                    where = pl.ds(lane * WIDE * TILE + k, TILE, stride=WIDE)
                    d_acc[where, :] = value[:, lane * 128 : (lane + 1) * 128]
            for half in range(2):
                firsts = [lane * WIDE * TILE + half * MID for lane in range(LANE_ROWS)]
                value = jnp.concatenate([d_acc[first : first + MID, :] for first in firsts], axis=1)
                store_unit(chunk * 2 + half, first, target, value)

        loop(left_count // TILE, body)
        flush(first, target)

    g_five = dot_nt(gp_six[:, columns(0)], w_eb[columns(0), :])
    for block in range(1, WIDE):
        g_five = g_five + dot_nt(gp_six[:, columns(block)], w_eb[columns(block), :])
    g_nar[...] = g_five
    back_activate(g_nar, z_five, 3, 7)
    send(7, 8)
    wide_weight_grad(lambda chunk: act_five[columns(chunk, TILE), :], MID, gp_six, ROW_EB, dwb)
    receive(7, 8)
    back_coefficients(7, 0, 1, 1, 3, 1.0)
    back_norm(g_nar, z_five, gp_nar, 3, 1)

    g_nar[...] = jnp.zeros(g_nar.shape, F32)

    def conv_b_back(step, tap):
        shift_into(gp_nar, 0, tap, shifted)
        g_nar[...] += dot_nt(shifted[...], tap_weight(tap))
        store_unit(step, ROW_SB, dwb, dot(act_four[...], shifted[...]), tap)

    low_two = (2 * 8 * counts[1] - ROW_SB) // MID if direct else 0
    conv_b_back(0, 8)
    flush_one(0, ROW_SB, dwb)
    sums_of((1, 3))
    loop(8 - low_two, lambda step: conv_b_back(step, 7 - step), 2)
    flush(ROW_SB, dwb)
    sums_of((1, 2))
    pump()
    loop(low_two, lambda step: conv_b_back(step, low_two - 1 - step), 2)
    get_sa.start()
    flush(ROW_SB, dwb)
    sums_of((1, 1))
    pump()
    back_activate(g_nar, z_four, 2, 8)
    send(8, 8)
    pump()
    receive(8, 8)
    back_coefficients(8, 0, 1, 1, 2, 1.0)
    back_norm(g_nar, z_four, gp_nar, 2, 1)
    pump()

    def middle_back(block):
        g_wide[:, columns(block)] += dot_nt(gp_nar[...], w_rb[columns(block), :])

    loop(WIDE, middle_back)
    pump()

    def join_step(here, block):
        main, side, value = joined_a(here, block)
        g = g_wide[here, columns(block)] * slope(value)
        g_wide[here, columns(block)] = g
        return (
            g,
            g * (main * row_of(4, 2, WIDE, block) + row_of(4, 3, WIDE, block)),
            g * (side * row_of(5, 2, WIDE, block) + row_of(5, 3, WIDE, block)),
        )

    each_sums(WIDE, join_step, 9, lambda block: (block, WIDE + block, 2 * WIDE + block))
    send(9, 16)
    pump()
    for kind in range(4):
        turn_over(act_one, 0, kind)

    def reduce_b_grad(block):
        store_unit(block, ROW_RB, dwb, dot_tn(middle[columns(block), :], gp_nar[...]))

    loop(WIDE, reduce_b_grad)
    flush(ROW_RB, dwb)
    sums_of((1, 0))
    pump()
    receive(9, 16)
    back_coefficients(9, 0, WIDE, WIDE, 4, 1.0)
    back_coefficients(9, 0, 2 * WIDE, WIDE, 5, 1.0)
    gp_main = cot_p
    back_norm(g_wide, z_main, gp_main, 4, WIDE)
    pump()
    g_nar[...] = dot_nt(gp_main[...], w_ea[...])
    back_activate(g_nar, z_two, 1, 10)
    send(10, 8)
    back_norm(g_wide, z_side, gp_side, 5, WIDE)
    pump()
    wide_weight_grad(lambda chunk: x_p[:, columns(chunk, TILE)].T, C_IN, gp_side, ROW_PA, dwa)
    sums_of((0, 3))
    pump()
    wide_weight_grad(lambda chunk: act_two[columns(chunk, TILE), :], MID, gp_main, ROW_EA, dwa)
    sums_of((0, 2))
    pump()
    receive(10, 8)
    back_coefficients(10, 0, 1, 1, 1, 1.0)
    back_norm(g_nar, z_two, gp_nar, 1, 1)
    pump()

    get_sa.wait()
    g_one = g_wide
    g_one[...] = jnp.zeros(g_one.shape, F32)

    def conv_a_back(tap):
        kind, table_row = strided_tap(tap)
        shift_into(gp_nar, 0, table_row, shifted)
        g_one[:, columns(kind)] += dot_nt(shifted[...], tap_weight(tap))

    for start in range(0, 9, 3):
        loop(3, lambda step, start=start: conv_a_back(start + step), 3)
        pump()
    back_activate(g_one, z_one, 0, 11)
    send(11, 8)
    pump()

    def conv_a_grad(step, tap):
        kind, table_row = strided_tap(tap)
        shift_into(gp_nar, 0, table_row, shifted)
        store_unit(step, ROW_SA, dwa, dot(act_one[:, columns(kind)], shifted[...]), tap)

    low_one = (8 * counts[0] - ROW_SA) // MID if direct else 0
    loop(9 - low_one, lambda step: conv_a_grad(step, 8 - step), 3)
    flush(ROW_SA, dwa)
    sums_of((0, 1))
    pump()
    if low_one:
        loop(low_one, lambda step: conv_a_grad(step, low_one - 1 - step), 3)
        flush(ROW_SA, dwa)
    pump()
    receive(11, 8)
    if direct:
        start_gains()
        for copy in flat_loads()[1:]:
            copy.start()
    back_coefficients(11, 0, 1, 1, 0, 4.0)
    gp_one = act_one
    back_norm(g_one, z_one, gp_one, 0, 1, same=True)

    for half in range(C_IN // MID):
        total = None
        for kind in range(4):
            left = x_p[:, kind * C_IN + half * MID : kind * C_IN + (half + 1) * MID]
            term = dot_tn(left, gp_one[:, columns(kind)])
            total = term if total is None else total + term
        store_unit(half, ROW_RA, dwa, total)
    flush(ROW_RA, dwa)
    sums_of((0, 0))
    pump()

    def image_back(kind):
        value = dot_nt(gp_one[:, columns(kind)], w_ra[...])
        x_p[:, columns(kind, C_IN)] = value.astype(BF16)

    x_side = dot_nt(gp_one[:, :MID], w_ra[...]) + dot_nt(gp_side[...], w_pa[...])
    x_p[:, :C_IN] = x_side.astype(BF16)
    for kind in range(1, 4):
        image_back(kind)
        pump()

    outs = (out_s, out_m, out_l)
    for res, (side, slots) in enumerate(layout.sizes):
        used = layout.tiles_of(res)
        here = slice(used[0] * TILE, (used[-1] + 1) * TILE)
        count = side * 2 * side * slots

        def scoped(raw, res=res, side=side, slots=slots, here=here, count=count):
            def copy_of(p):
                return pltpu.make_async_copy(raw.at[p], outs[res].at[:, p], isem.at[p])

            for p in range(2):
                row = 2 * res + p
                for block in range(C_IN // MID):
                    total = None
                    for q in range(2):
                        lanes = codes_back[row : row + 1, q * rows + here.start : q * rows + here.stop]
                        first = (2 * p + q) * C_IN + block * MID
                        term = dot(one_hot(lanes, count), x_p[here, first : first + MID])
                        total = term if total is None else total + term
                    total = total.astype(BF16).reshape(side, 2 * side, slots, MID)
                    raw[p, :, :, :, block * MID : (block + 1) * MID] = total
                copy_of(p).start()
                pump()
            for p in range(2):
                copy_of(p).wait()

        pl.run_scoped(scoped, pltpu.VMEM((2, side, 2 * side, slots, C_IN), BF16))

    if not direct:
        return
    pump(len(pending))
    for i in range(2):
        last_sum(i, share_at[i])
    flat_loads()[0].start()
    for i in range(2):
        layer_squares(i, d_acc, share_at[i], 8)
    r.norms[15:16, :] = jnp.full((1, 128), local_pixels, F32)
    update()

    for i in range(2):
        for zz in range(groups):
            for k in range(len(spread_plan)):
                spread(i, zz, k).wait_send()
            for k in range(4):
                piece(i, zz, 0, k).wait_send()

            @pl.when(zz != me_x)
            def _(i=i, zz=zz):
                to_z(i, zz).wait_send()

    for u in range(len(sum_order) - len(work), len(sum_order)):
        for k in range(4, 10):
            piece(*sum_order[u], u % len(work), k).wait_send()


def both_blocks(groups, direct, images, cots, wa, wb, gains, counts, moments):
    layout = Layout([image.shape for image in images])
    rows = layout.rows
    img_codes = layout.picture_rows(2)
    cot_codes = layout.picture_rows(1)

    def by_pixel(picture, step):
        turned = jnp.transpose(picture, (1, 2, 0, 3))
        return turned.reshape(turned.shape[0] // step, step, *turned.shape[1:])

    def table(codes):
        width = round_up(max(code.shape[0] for code in codes), 128)
        result = np.full((round_up(len(codes), 8), width), -1, np.int32)
        for index, code in enumerate(codes):
            result[index, : code.shape[0]] = code
        return jnp.asarray(result)

    back = layout.picture_back()
    back = np.concatenate([back, np.full((round_up(len(back), 8) - len(back), back.shape[1]), -1, np.int32)])
    anywhere = pl.BlockSpec(memory_space=pl.ANY)
    vmem = pl.BlockSpec(memory_space=pltpu.VMEM)
    wide16 = pltpu.VMEM((rows, C_OUT), BF16)
    wide32 = pltpu.VMEM((rows, C_OUT), F32)
    nar16 = pltpu.VMEM((rows, MID), BF16)
    nar32 = pltpu.VMEM((rows, MID), F32)
    shapes = [
        *[jax.ShapeDtypeStruct(by_pixel(image, 2).shape, BF16) for image in images],
        jax.ShapeDtypeStruct((END_A, MID), BF16),
        jax.ShapeDtypeStruct((END_B, MID), BF16),
        jax.ShapeDtypeStruct((EXCHANGES, 16, MID), F32),
    ]
    scratch = [
        *[wide16, wide16, wide16, pltpu.VMEM((WIDE * rows, MID), BF16), wide32],
        pltpu.VMEM((WIDE * rows, MID), BF16),
        *[wide16] * 3,
        *[nar32] * 4,
        *[nar16] * 5,
        pltpu.VMEM((rows, 4 * C_IN), BF16),
        pltpu.VMEM((C_IN, MID), BF16),
        pltpu.VMEM((9 * MID, MID), BF16),
        pltpu.VMEM((MID, C_OUT), BF16),
        pltpu.VMEM((C_IN, C_OUT), BF16),
        pltpu.VMEM((C_OUT, MID), BF16),
        pltpu.VMEM((C_OUT, MID), BF16),
        pltpu.VMEM((LANE_ROWS * WIDE * TILE, 128), F32),
        pltpu.VMEM((2 * MID, MID), BF16),
        pltpu.VMEM((SUM_ROWS, MID), F32),
        pltpu.VMEM((groups, SUM_ROWS, MID), F32),
        pltpu.VMEM((16, 16, MID), F32),
        pltpu.VMEM((rows, 1), F32),
        pltpu.SemaphoreType.DMA((5,)),
        pltpu.SemaphoreType.DMA((2 * MID // TILE,)),
        pltpu.SemaphoreType.DMA((2,)),
        pltpu.SemaphoreType.DMA((len(images),)),
        pltpu.SemaphoreType.DMA((EXCHANGES, groups - 1)),
        pltpu.SemaphoreType.DMA((EXCHANGES, groups - 1)),
    ]
    names = INPUTS + (DIRECT_INPUTS if direct else []) + OUTPUTS
    places = [anywhere] * 5 + [vmem]
    if direct:
        count_a, count_b = wa.shape[0] // LANE_ROWS, wb.shape[0] // LANE_ROWS
        names = names + DIRECT_OUTPUTS
        shapes += [jax.ShapeDtypeStruct(value.shape, F32) for value in (wa, wb, *gains)]
        shapes += [jax.ShapeDtypeStruct((7, 2), F32)]
        shapes += [jax.ShapeDtypeStruct((count, MID), BF16) for count in (END_A, END_B)]
        for per in (4, 2, 1, 1):
            shapes += [jax.ShapeDtypeStruct((groups * per * n, MID), BF16) for n in (count_a, count_b)]
        places += [anywhere] * 2 + [vmem] * 3 + [anywhere] * (len(DIRECT_OUTPUTS) - 5)
        scratch += [
            pltpu.VMEM((4 * count_a, MID), BF16),
            pltpu.VMEM((2 * count_a, MID), BF16),
            pltpu.VMEM((count_a, MID), BF16),
            pltpu.VMEM((groups * count_b, MID), BF16),
            pltpu.VMEM((LANE_ROWS * (count_a + 2 * count_b), 128), F32),
            pltpu.VMEM((32, MID), F32),
            pltpu.VMEM((8, 32, MID), F32),
            pltpu.VMEM((16, 128), F32),
            pltpu.VMEM((groups, 16, 128), F32),
            pltpu.VMEM((8, 16, 128), F32),
            pltpu.SemaphoreType.DMA((8,)),
            pltpu.SemaphoreType.DMA((2 * groups, 9)),
            pltpu.SemaphoreType.DMA((2 * groups, 9)),
            pltpu.SemaphoreType.DMA((2, groups - 1)),
            pltpu.SemaphoreType.DMA((2, groups)),
            pltpu.SemaphoreType.DMA((2 * groups, 11)),
            pltpu.SemaphoreType.DMA((2 * groups, 11)),
            pltpu.SemaphoreType.DMA((4,)),
            pltpu.SemaphoreType.DMA((7,)),
            pltpu.SemaphoreType.DMA((7,)),
            pltpu.SemaphoreType.DMA((groups - 1,)),
            pltpu.SemaphoreType.DMA((groups - 1,)),
            pltpu.SemaphoreType.DMA((7,)),
            pltpu.SemaphoreType.DMA((7,)),
        ]
    names = names + SCRATCH + (DIRECT_SCRATCH if direct else [])
    out = pl.pallas_call(
        functools.partial(mega, names, layout, groups, direct),
        out_shape=shapes,
        in_specs=[anywhere] * 8
        + [vmem] * 7
        + [pl.BlockSpec(memory_space=pltpu.SMEM)]
        + ([anywhere] * 2 + [vmem] * 2 if direct else []),
        out_specs=places,
        scratch_shapes=scratch,
        compiler_params=pltpu.CompilerParams(
            collective_id=0, has_side_effects=True, vmem_limit_bytes=125 * 512 * 1024
        ),
    )(
        *[by_pixel(image, 2) for image in images],
        *[by_pixel(cot, 1) for cot in cots],
        wa,
        wb,
        *gains,
        jnp.asarray(layout.neighbours()),
        table(img_codes),
        table(cot_codes),
        jnp.asarray(back),
        jnp.asarray(layout.row_codes()),
        counts,
        *(moments if direct else ()),
    )
    image_grads = [
        jnp.transpose(grad.reshape(-1, *grad.shape[2:]), (2, 0, 1, 3)) for grad in out[: len(images)]
    ]
    return (*image_grads, *out[len(images) :])


def layer_masks(first, count, bounds):
    position = first + jnp.arange(count, dtype=jnp.int32)
    rows = [(position >= low) & (position < high) for low, high in zip(bounds[:-1], bounds[1:])]
    return jnp.stack(rows).astype(F32)


def body(
    image_small,
    image_medium,
    image_large,
    cot_small,
    cot_medium,
    cot_large,
    counts,
    weights_a,
    weights_b,
    moment_a,
    moment_b,
    gains_narrow,
    gains_wide,
    gain_moment_narrow,
    gain_moment_wide,
):
    images = (image_small, image_medium, image_large)
    cots = (cot_small, cot_medium, cot_large)
    groups = lax.axis_size("gx")
    rows_a = weights_a.shape[0] // MID
    rows_b = weights_b.shape[0] // MID
    gains = (gains_narrow, gains_wide)
    direct = groups == 4 and lax.axis_size("gy") == 8 and rows_a % 16 == 0 and rows_b % 16 == 0
    if direct:
        flats = [value.reshape(-1, 128) for value in (weights_a, weights_b, moment_a, moment_b)]
        moments = (*flats[2:], gain_moment_narrow, gain_moment_wide)
        out = both_blocks(groups, direct, images, cots, *flats[:2], gains, counts, moments)
        return (*out[:3], out[6].reshape(-1), out[7].reshape(-1), *out[8:11])
    sides = [image.shape[1] // 2 for image in images]
    local_pixels = sum(counts[0, r] * sides[r] ** 2 for r in range(3)).astype(F32)
    flat_a = weights_a.reshape(rows_a, MID)
    flat_b = weights_b.reshape(rows_b, MID)
    wa = lax.all_gather(flat_a.astype(BF16), ("gx", "gy"), axis=0, tiled=True)
    wb = lax.all_gather(flat_b.astype(BF16), ("gx", "gy"), axis=0, tiled=True)
    out = both_blocks(groups, direct, images, cots, wa, wb, gains, counts, ())
    image_grads, (dwa, dwb, totals) = out[:3], out[3:6]

    def scattered(grads):
        return lax.psum_scatter(grads, ("gx", "gy"), scatter_dimension=0, tiled=True).astype(F32)

    share_a, share_b = scattered(dwa), scattered(dwb)
    device = lax.axis_index(("gx", "gy"))
    masks_a = layer_masks(device * rows_a, rows_a, [ROW_RA, ROW_SA, ROW_EA, ROW_PA, END_A])
    masks_b = layer_masks(device * rows_b, rows_b, [ROW_RB, ROW_SB, ROW_EB, END_B])

    def layer_squares(masks, flat):
        return jnp.sum(masks * jnp.sum(flat * flat, axis=1)[None, :], axis=1)

    weight_squares = jnp.concatenate([layer_squares(masks_a, flat_a), layer_squares(masks_b, flat_b)])
    grad_squares = jnp.concatenate([layer_squares(masks_a, share_a), layer_squares(masks_b, share_b)])
    partial_norms = jnp.stack([weight_squares, grad_squares], axis=1)

    def narrow(e):
        return jnp.stack([totals[e, 1], totals[e, 0]])

    def wide(e, cross):
        return jnp.stack(
            [totals[e, cross : cross + WIDE].reshape(-1), totals[e, :WIDE].reshape(-1)]
        )

    sums_narrow = jnp.stack([narrow(11), narrow(10), narrow(8), narrow(7)])
    sums_wide = jnp.stack([wide(9, WIDE), wide(9, 2 * WIDE), wide(6, WIDE)])
    total_narrow, total_wide = lax.psum((sums_narrow, sums_wide), "gy")
    total_norms, pixels_total = lax.psum((partial_norms, local_pixels), ("gx", "gy"))
    weight_norm = jnp.sqrt(total_norms[:, 0])
    grad_norm = jnp.sqrt(total_norms[:, 1]) / pixels_total
    trust_ratio = TRUST_SCALE * weight_norm / (grad_norm + WEIGHT_DECAY * weight_norm)

    def update(masks, trust, share, flat, moment):
        trust_rows = jnp.sum(masks * trust[:, None], axis=0)[:, None]
        step = LEARN_RATE * trust_rows * (share / pixels_total + WEIGHT_DECAY * flat)
        return MOMENTUM * moment + step.reshape(-1)

    return (
        *image_grads,
        update(masks_a, trust_ratio[:4], share_a, flat_a, moment_a),
        update(masks_b, trust_ratio[4:], share_b, flat_b, moment_b),
        MOMENTUM * gain_moment_narrow + GAIN_RATE * (total_narrow / pixels_total),
        MOMENTUM * gain_moment_wide + GAIN_RATE * (total_wide / pixels_total),
        jnp.stack([weight_norm, grad_norm], axis=1),
    )


def solution(mesh):
    split = P(("gx", "gy"))
    in_specs = (split,) * 11 + (P(),) * 4
    out_specs = (split,) * 5 + (P(),) * 3
    return jax.shard_map(body, mesh=mesh, in_specs=in_specs, out_specs=out_specs, check_vma=False)
```

```python
import functools

import jax
import jax.numpy as jnp
import numpy as np
from jax import lax
from jax.experimental import pallas as pl
from jax.experimental.pallas import tpu as pltpu
from jax.sharding import PartitionSpec as P

C_IN = 1024
MID = 512
C_OUT = 2048

EPSILON = 1e-05
MOMENTUM = 0.9
LEARN_RATE = 20.0
TRUST_SCALE = 0.001
WEIGHT_DECAY = 5e-05
GAIN_RATE = 0.2

MESH = pl.DeviceIdType.MESH
F32 = jnp.float32
BF16 = jnp.bfloat16
TILE = 256
ROWS = 64
WIDE = C_OUT // MID
LANE_ROWS = MID // 128

ROW_RA, ROW_SA, ROW_EA, ROW_PA = 0, C_IN, C_IN + 9 * MID, C_IN + 9 * MID + C_OUT
END_A = ROW_PA + C_IN * WIDE
ROW_RB, ROW_SB, ROW_EB = 0, C_OUT, C_OUT + 9 * MID
END_B = ROW_EB + C_OUT

EXCHANGES = 12
FIRST = [8 * e + 8 * sum(wide < e for wide in (2, 9)) for e in range(EXCHANGES)]
SUM_ROWS = 8 * (EXCHANGES + 2)


GATHER_STEPS = (
    (("near", 0, 0),),
    (("far", 0, 0), ("near", 1, 0), ("own", 0, 1)),
    (("far", 1, 0), ("near", 0, 1), ("own", 0, 2)),
    (("far", 0, 1), ("near", 0, 2), ("own", 0, 3)),
    (("far", 0, 2),),
    (("own", 1, 1), ("near", 0, 3)),
    (),
    (),
    (),
    (("far", 0, 3), ("own", 1, 2), ("own", 1, 3), ("near", 1, 1)),
    (),
    (("far", 1, 1), ("near", 1, 2)),
    (("near", 1, 3), ("far", 1, 2)),
    (),
    (("far", 1, 3),),
)


def round_up(value, unit):
    return -(-value // unit) * unit


class Layout:
    def __init__(self, shapes):
        pictures = [
            (shape[1] // 2, res, slot)
            for res, shape in enumerate(shapes)
            for slot in range(shape[0])
        ]
        self.sizes = [(shape[1] // 2, shape[0]) for shape in shapes]
        pictures.sort(key=lambda item: (-item[0], item[2]))
        self.tiles = []
        self.fill = []
        for side, res, slot in pictures:
            for tile in range(len(self.tiles) + 1):
                if tile == len(self.tiles):
                    self.tiles.append([])
                    self.fill.append(0)
                if self.fill[tile] + side * side <= TILE:
                    self.tiles[tile].append((side, res, slot, self.fill[tile]))
                    self.fill[tile] += side * side
                    break
        self.rows = TILE * len(self.tiles)

    def row_codes(self):
        codes = np.full((self.rows, 1), -1, np.int32)
        for tile, members in enumerate(self.tiles):
            for side, res, slot, start in members:
                first = tile * TILE + start
                codes[first : first + side * side] = (res << 16) + slot
        return codes

    def neighbours(self):
        table = np.full((16, self.rows), -1, np.int32)
        for tap in range(9):
            down, right = tap // 3 - 1, tap % 3 - 1
            for tile, members in enumerate(self.tiles):
                for side, _, _, start in members:
                    for i in range(side):
                        for j in range(side):
                            if 0 <= i + down < side and 0 <= j + right < side:
                                table[tap, tile * TILE + start + i * side + j] = (
                                    start + (i + down) * side + j + right
                                )
        return table

    def picture_rows(self, step):
        result = []
        for members in self.tiles:
            for res, (side, slots) in enumerate(self.sizes):
                codes = np.full((step, side, side * step, slots), -1, np.int32)
                for member_side, member_res, slot, start in members:
                    if member_res == res:
                        for i in range(side):
                            for c in range(side * step):
                                for p in range(step):
                                    row = start + i * side + c // step
                                    codes[p, i, c, slot] = (2 * p + c % step) * TILE + row
                result += [codes[p].reshape(-1) for p in range(step)]
        return result

    def picture_back(self):
        result = []
        for res, (side, slots) in enumerate(self.sizes):
            for p in range(2):
                back = np.full((2, self.rows), -1, np.int32)
                for tile, members in enumerate(self.tiles):
                    for member_side, member_res, slot, start in members:
                        if member_res == res:
                            for i in range(side):
                                for c in range(2 * side):
                                    row = tile * TILE + start + i * side + c // 2
                                    back[c % 2, row] = (i * 2 * side + c) * slots + slot
                result += [back.reshape(-1)]
        return np.stack(result)

    def tiles_of(self, res):
        return [tile for tile, members in enumerate(self.tiles) if any(m[1] == res for m in members)]


def dot(left, right):
    return jnp.dot(left, right, preferred_element_type=F32)


def dot_tn(left, right):
    return lax.dot_general(left, right, (((0,), (0,)), ((), ())), preferred_element_type=F32)


def dot_nt(left, right):
    return lax.dot_general(left, right, (((1,), (1,)), ((), ())), preferred_element_type=F32)


def sigmoid(value):
    return 0.5 * jnp.tanh(0.5 * value) + 0.5


def one_hot(targets, count, offset=0):
    ids = lax.broadcasted_iota(jnp.int32, (count, targets.shape[1]), 0) + offset
    return jnp.where(ids == targets, 1.0, 0.0).astype(BF16)


def loop(count, body, unroll=1):
    def step(index, carry):
        body(index)
        return carry

    lax.fori_loop(0, count, step, 0, unroll=unroll)


def columns(index, width=MID):
    if isinstance(index, int):
        return pl.ds(index * width, width)
    return pl.ds(pl.multiple_of(index * width, width), width)


INPUTS = [
    "img_s",
    "img_m",
    "img_l",
    "cot_s",
    "cot_m",
    "cot_l",
    "wa",
    "wb",
    "gains_n",
    "gains_w",
    "shifts",
    "codes_img",
    "codes_cot",
    "codes_back",
    "codes_row",
    "counts_in",
]
DIRECT_INPUTS = [
    "moment_a",
    "moment_b",
    "gain_moment_n",
    "gain_moment_w",
]
SCRATCH = [
    "z_one",
    "z_main",
    "z_side",
    "z_six",
    "g_wide",
    "middle",
    "cot_p",
    "gp_side",
    "act_one",
    "z_two",
    "z_four",
    "z_five",
    "g_nar",
    "act_two",
    "act_four",
    "act_five",
    "gp_nar",
    "shifted",
    "x_p",
    "w_ra",
    "w_sp",
    "w_ea",
    "w_pa",
    "w_rb",
    "w_eb",
    "d_acc",
    "d_out",
    "stats",
    "arrived",
    "par",
    "mask",
    "wsem",
    "rsem",
    "dsem",
    "isem",
    "xsend",
    "xrecv",
]
OUTPUTS = [
    "out_s",
    "out_m",
    "out_l",
    "dwa",
    "dwb",
    "totals",
]
DIRECT_OUTPUTS = [
    "new_a",
    "new_b",
    "new_gain_n",
    "new_gain_w",
    "norms_out",
    "all_a",
    "all_b",
    "r1_a",
    "r1_b",
    "r2_a",
    "r2_b",
    "r3_a",
    "r3_b",
    "r4_a",
    "r4_b",
]
DIRECT_SCRATCH = [
    "in_one",
    "in_two",
    "in_three",
    "part_b",
    "flat",
    "gain_sums",
    "gain_got",
    "norms",
    "norm_got",
    "norm_all",
    "lsem",
    "gsend",
    "grecv",
    "fsend",
    "frecv",
    "ssend",
    "srecv",
    "hsem",
    "asend",
    "arecv",
    "bsend",
    "brecv",
    "csend",
    "crecv",
]


class Named:
    def __init__(self, names, refs):
        self.__dict__.update(zip(names, refs, strict=True))


def mega(names, layout, groups, direct, *refs):
    r = Named(names, refs)
    img_s = r.img_s
    img_m = r.img_m
    img_l = r.img_l
    cot_s = r.cot_s
    cot_m = r.cot_m
    cot_l = r.cot_l
    wa = r.wa
    wb = r.wb
    codes_row = r.codes_row
    counts_in = r.counts_in
    mask = r.mask
    gains_n = r.gains_n
    gains_w = r.gains_w
    shifts = r.shifts
    codes_img = r.codes_img
    codes_cot = r.codes_cot
    codes_back = r.codes_back
    out_s = r.out_s
    out_m = r.out_m
    out_l = r.out_l
    dwa = r.dwa
    dwb = r.dwb
    totals = r.totals
    z_one = r.z_one
    z_main = r.z_main
    z_side = r.z_side
    z_six = r.z_six
    g_wide = r.g_wide
    middle = r.middle
    cot_p = r.cot_p
    gp_side = r.gp_side
    act_one = r.act_one
    z_two = r.z_two
    z_four = r.z_four
    z_five = r.z_five
    g_nar = r.g_nar
    act_two = r.act_two
    act_four = r.act_four
    act_five = r.act_five
    gp_nar = r.gp_nar
    shifted = r.shifted
    x_p = r.x_p
    w_ra = r.w_ra
    w_sp = r.w_sp
    w_ea = r.w_ea
    w_pa = r.w_pa
    w_rb = r.w_rb
    w_eb = r.w_eb
    d_acc = r.d_acc
    d_out = r.d_out
    stats = r.stats
    arrived = r.arrived
    par = r.par
    wsem = r.wsem
    rsem = r.rsem
    dsem = r.dsem
    isem = r.isem
    xsend = r.xsend
    xrecv = r.xrecv
    rows = layout.rows
    tiles = len(layout.tiles)
    steps = rows // ROWS
    me_x = lax.axis_index("gx")
    me_y = lax.axis_index("gy")

    y, x, core = me_y // 4, (me_y // 2) % 2, me_y % 2
    to_x = (y * 2 + 1 - x) * 2 + core
    to_y = ((1 - y) * 2 + x) * 2 + core
    across = ((1 - y) * 2 + 1 - x) * 2 + core
    twin = (y * 2 + x) * 2 + 1 - core

    barrier = pltpu.get_barrier_semaphore()
    greeted = [(lax.rem(me_x + hop, groups), me_y) for hop in range(1, groups)]
    if direct:
        greeted += [(me_x, lax.rem(me_y + hop, 8)) for hop in range(1, 8)]
    for device in greeted:
        pl.semaphore_signal(barrier, inc=1, device_id=device, device_id_type=MESH)

    if direct:
        counts = (wa.shape[0] // LANE_ROWS, wb.shape[0] // LANE_ROWS)
        shards = (r.in_three, r.in_two.at[pl.ds(0, counts[1])])
    else:
        counts = (wa.shape[0], wb.shape[0])
    halves = (counts[0] - counts[0] // 32 * 16, counts[1] // 32 * 16)
    if direct:
        full_a, full_b = r.all_a, r.all_b
    else:
        full_a, full_b = wa, wb
    alls = (full_a, full_b)

    def span(first, count):
        return pl.ds(first if isinstance(first, int) else pl.multiple_of(first, 16), count)

    def part_of(i, which):
        count, cut = counts[i], halves[i]
        return {"low": (0, cut), "high": (cut, count - cut), "all": (0, count)}[which]

    def remote(source, target, send_sem, recv_sem, device):
        return pltpu.make_async_remote_copy(
            src_ref=source,
            dst_ref=target,
            send_sem=send_sem,
            recv_sem=recv_sem,
            device_id=device,
            device_id_type=MESH,
        )

    def along_z(i, hop):
        here = alls[i].at[span((me_x * 8 + me_y) * counts[i], counts[i])]
        device = (lax.rem(me_x + hop, groups), me_y)
        return remote(shards[i], here, r.fsend.at[i, hop - 1], r.frecv.at[i, me_x], device)

    def from_z(i, zz):
        here = alls[i].at[span((zz * 8 + me_y) * counts[i], counts[i])]
        return remote(shards[i], here, r.fsend.at[i, 0], r.frecv.at[i, zz], (me_x, me_y))

    spread_plan = (
        (me_y, "all", to_x),
        (me_y, "all", to_y),
        (me_y, "all", twin),
        (to_x, "low", to_y),
        (to_x, "all", twin),
        (to_y, "high", to_x),
        (to_y, "all", twin),
        (across, "low", twin),
        (across, "high", twin),
    )

    def spread(i, zz, k):
        owner, which, target = spread_plan[k]
        low, count = part_of(i, which)
        here = alls[i].at[span((zz * 8 + owner) * counts[i] + low, count)]
        unit = i * 4 + zz
        return remote(here, here, r.gsend.at[unit, k], r.grecv.at[unit, k], (me_x, target))

    def spread_own(i, zz):
        @pl.when(zz != me_x)
        def _():
            from_z(i, zz).wait_recv()

        for k in (0, 1, 2):
            spread(i, zz, k).start()

    def spread_near(i, zz):
        for got, onward in ((0, (3, 4)), (1, (5, 6))):
            spread(i, zz, got).wait_recv()
            for k in onward:
                spread(i, zz, k).start()

    def spread_far(i, zz):
        for got, onward in ((3, 7), (5, 8)):
            spread(i, zz, got).wait_recv()
            spread(i, zz, onward).start()

    def spread_done(i, zz):
        for k in (2, 4, 6, 7, 8):
            spread(i, zz, k).wait_recv()

    def turn(k):
        return me_x if k == 0 else k - 1 + (k + 3 - me_x) // 4

    def own(i, k):
        if direct:
            spread_own(i, turn(k))

    def pass_on(place):
        if direct:
            for step in GATHER_STEPS[place]:
                {"own": spread_own, "near": spread_near, "far": spread_far}[step[0]](step[1], turn(step[2]))

    def done(i, zz):
        if direct:
            spread_done(i, zz)

    def fetch(source, first, count, target, sem):
        return pltpu.make_async_copy(source.at[pl.ds(first, count)], target, wsem.at[sem])

    cut = min(max(8 * counts[0] - ROW_SA, 0), 9 * MID) if direct else 4 * MID
    get_ra = fetch(full_a, ROW_RA, C_IN, w_ra, 0)
    get_sa_low = fetch(full_a, ROW_SA, cut, w_sp.at[pl.ds(0, cut)], 1)
    get_sa_high = fetch(full_a, ROW_SA + cut, 9 * MID - cut, w_sp.at[pl.ds(cut, 9 * MID - cut)], 4)
    get_sa = fetch(full_a, ROW_SA, 9 * MID, w_sp, 1)
    get_rb = fetch(full_b, ROW_RB, C_OUT, w_rb, 2)
    get_sb = fetch(full_b, ROW_SB, 9 * MID, w_sp, 3)

    dws = (dwa, dwb)
    if direct:
        r_one, r_two, r_three = (r.r1_a, r.r1_b), (r.r2_a, r.r2_b), (r.r3_a, r.r3_b)
        r_four, parts = (r.r4_a, r.r4_b), (w_rb, r.part_b)
    work = (z_six, w_eb, middle)

    def piece(i, zz, slot, which_one):
        count, unit = counts[i], i * 4 + zz
        low, low_count = part_of(i, "low")
        high, high_count = part_of(i, "high")
        at = work[slot].at
        plan = []
        for q in range(4):
            source = dws[i].at[span((zz * 8 + q * 2 + 1 - core) * count, count)]
            plan.append((source, r_one[i].at[span((zz * 4 + q) * count, count)], twin))
        for k in range(2):
            source = at[span((k * 2 + 1 - x) * count + low, low_count)]
            plan.append((source, r_two[i].at[span((zz * 2 + k) * count + low, low_count)], to_x))
        for k in range(2):
            source = at[span(((1 - y) * 2 + k) * count + high, high_count)]
            plan.append((source, r_two[i].at[span((zz * 2 + k) * count + high, high_count)], to_y))
        source = at[span(((1 - y) * 2 + x) * count + low, low_count)]
        plan.append((source, r_three[i].at[span(zz * count + low, low_count)], to_y))
        source = at[span((y * 2 + 1 - x) * count + high, high_count)]
        plan.append((source, r_three[i].at[span(zz * count + high, high_count)], to_x))
        source, target, device = plan[which_one]
        sems = r.ssend.at[unit, which_one], r.srecv.at[unit, which_one]
        return remote(source, target, *sems, (me_x, device))

    def local(source, target, sem):
        return pltpu.make_async_copy(source, target, r.lsem.at[sem])

    def loads_one(i, zz, slot):
        count = counts[i]
        result = [
            local(
                dws[i].at[span((zz * 8 + q * 2 + core) * count, count)],
                work[slot].at[span(q * count, count)],
                q,
            )
            for q in range(4)
        ]
        arrivals = r_one[i].at[span(zz * 4 * count, 4 * count)]
        return result + [local(arrivals, r.in_one.at[span(0, 4 * count)], 4)]

    def load_two(i, zz):
        count = 2 * counts[i]
        return local(r_two[i].at[span(zz * count, count)], r.in_two.at[span(0, count)], 5)

    def load_three(i, zz):
        count = counts[i]
        return local(r_three[i].at[span(zz * count, count)], r.in_three.at[span(0, count)], 6)

    def add_rows(target, target_first, left, left_first, right, right_first, count):
        step = 32 if count % 32 == 0 else 16

        def body(index):
            def at(first):
                return span(first + index * step, step)

            total = left[at(left_first), :].astype(F32) + right[at(right_first), :].astype(F32)
            target[at(target_first), :] = total.astype(BF16)

        loop(count // step, body, unroll=2)

    def sum_send(i, zz, slot):
        for k in range(4):
            piece(i, zz, slot, k).start()

    def sum_one_load(i, zz, slot, before):
        if before is not None:
            for k in range(4, 10):
                piece(before[0], before[1], slot, k).wait_send()
        for k in range(4):
            piece(i, zz, slot, k).wait_recv()
        for copy in loads_one(i, zz, slot):
            copy.start()

    def sum_one(i, zz, slot):
        for copy in loads_one(i, zz, slot):
            copy.wait()
        add_rows(work[slot], 0, work[slot], 0, r.in_one, 0, 4 * counts[i])
        for k in range(4, 8):
            piece(i, zz, slot, k).start()

    def sum_two_load(i, zz, slot):
        for k in range(4, 8):
            piece(i, zz, slot, k).wait_recv()
        load_two(i, zz).start()

    def sum_two(i, zz, slot):
        load_two(i, zz).wait()
        count = counts[i]
        low, low_count = part_of(i, "low")
        high, high_count = part_of(i, "high")
        for k in range(2):
            first = (k * 2 + x) * count + low
            add_rows(work[slot], first, work[slot], first, r.in_two, k * count + low, low_count)
            first = (y * 2 + k) * count + high
            add_rows(work[slot], first, work[slot], first, r.in_two, k * count + high, high_count)
        for k in range(8, 10):
            piece(i, zz, slot, k).start()

    def sum_three_load(i, zz, slot):
        for k in range(8, 10):
            piece(i, zz, slot, k).wait_recv()
        load_three(i, zz).start()

    def to_z(i, zz):
        count = counts[i]
        return remote(
            parts[i].at[span(zz * count, count)],
            r_four[i].at[span(me_x * count, count)],
            r.ssend.at[i * 4 + zz, 10],
            r.srecv.at[i * 4 + me_x, 10],
            (zz, me_y),
        )

    def sum_three(i, zz, slot):
        load_three(i, zz).wait()
        count = counts[i]
        mine = (y * 2 + x) * count
        add_rows(parts[i], zz * count, work[slot], mine, r.in_three, 0, count)

        @pl.when(zz != me_x)
        def _():
            to_z(i, zz).start()

    def last_sum(i, share):
        count = counts[i]

        def arrived_from(zz):
            here = span(zz * count, count)
            return remote(
                parts[i].at[here], r_four[i].at[here], r.ssend.at[i * 4, 10], r.srecv.at[i * 4 + zz, 10], (me_x, me_y)
            )

        def load(zz):
            here = span(zz * count, count)
            return local(r_four[i].at[here], r.in_one.at[here], zz)

        for zz in range(groups):

            @pl.when(zz != me_x)
            def _():
                arrived_from(zz).wait_recv()
                load(zz).start()

        for zz in range(groups):

            @pl.when(zz != me_x)
            def _():
                load(zz).wait()

            @pl.when(zz == me_x)
            def _():
                r.in_one[span(zz * count, count), :] = parts[i][span(zz * count, count), :]

        total = r.in_one[0:count, :].astype(F32)
        for zz in range(1, groups):
            total = total + r.in_one[zz * count : (zz + 1) * count, :].astype(F32)
        put_flat(total, share, count)

    device = me_x * 8 + me_y
    flat_rows = tuple(LANE_ROWS * count for count in counts)
    layer_bounds = tuple(
        tuple(row * LANE_ROWS for row in bounds)
        for bounds in ((ROW_RA, ROW_SA, ROW_EA, ROW_PA, END_A), (ROW_RB, ROW_SB, ROW_EB, END_B))
    )
    layers_before = (0, len(layer_bounds[0]) - 1)
    share_at = (0, flat_rows[0])
    weight_at = ((d_acc, flat_rows[0] + flat_rows[1] + 32), (r.flat, 0)) if direct else None
    moment_at = (flat_rows[1], flat_rows[1] + flat_rows[0])
    FLAT_STEP = 64

    def put_flat(value, first, count):
        for lane in range(LANE_ROWS):
            part = value[:, lane * 128 : (lane + 1) * 128]
            d_acc[pl.ds(first + lane, count, stride=LANE_ROWS), :] = part

    def in_layer(i, step, layer):
        ids = lax.broadcasted_iota(jnp.int32, (FLAT_STEP, 128), 0) + (device * flat_rows[i] + step * FLAT_STEP)
        return (ids >= layer_bounds[i][layer]) & (ids < layer_bounds[i][layer + 1])

    def layer_squares(i, ref, first, norm_row):
        layers = len(layer_bounds[i]) - 1

        def step(index, sums):
            value = ref[pl.ds(pl.multiple_of(first + index * FLAT_STEP, 32), FLAT_STEP), :]
            square = value * value
            return tuple(
                kept
                + jnp.sum(
                    jnp.where(in_layer(i, index, layer), square, 0.0).reshape(FLAT_STEP // 8, 8, 128), axis=0
                )
                for layer, kept in enumerate(sums)
            )

        start = tuple(jnp.zeros((8, 128), F32) for _ in range(layers))
        sums = lax.fori_loop(0, flat_rows[i] // FLAT_STEP, step, start)
        for layer, value in enumerate(sums):
            row = norm_row + layers_before[i] + layer
            r.norms[row : row + 1, :] = jnp.sum(value, axis=0, keepdims=True)

    def swap_all(axis_size, source, target, slot, device_of, send_sems, recv_sems):
        return [
            remote(source, target.at[slot], send_sems.at[hop - 1], recv_sems.at[hop - 1], device_of(hop))
            for hop in range(1, axis_size)
        ]

    def gain_swap():
        return swap_all(
            8, r.gain_sums, r.gain_got, me_y, lambda hop: (me_x, lax.rem(me_y + hop, 8)), r.asend, r.arecv
        )

    def norm_swap_x():
        return swap_all(
            groups,
            r.norms,
            r.norm_got,
            me_x,
            lambda hop: (lax.rem(me_x + hop, groups), me_y),
            r.bsend,
            r.brecv,
        )

    def norm_swap_y():
        return swap_all(
            8, r.norms, r.norm_all, me_y, lambda hop: (me_x, lax.rem(me_y + hop, 8)), r.csend, r.crecv
        )

    def start_gains():
        rows_of = []
        for e in (11, 10, 8, 7):
            rows_of += [(e, 1), (e, 0)]
        for e, cross in ((9, WIDE), (9, 2 * WIDE), (6, WIDE)):
            rows_of += [(e, cross + j) for j in range(WIDE)] + [(e, j) for j in range(WIDE)]
        for row, (e, source) in enumerate(rows_of):
            r.gain_sums[row : row + 1, :] = totals[e, source : source + 1, :]
        for copy in gain_swap():
            copy.start()
        r.gain_got[pl.ds(me_y, 1)] = r.gain_sums[...][None]

    def flat_loads():
        return [
            pltpu.make_async_copy(wa, d_acc.at[pl.ds(weight_at[0][1], flat_rows[0])], r.hsem.at[0]),
            pltpu.make_async_copy(wb, r.flat.at[pl.ds(0, flat_rows[1])], r.hsem.at[1]),
            pltpu.make_async_copy(r.moment_a, r.flat.at[pl.ds(moment_at[0], flat_rows[0])], r.hsem.at[2]),
            pltpu.make_async_copy(r.moment_b, r.flat.at[pl.ds(moment_at[1], flat_rows[1])], r.hsem.at[3]),
        ]

    def update():
        for copy in norm_swap_x():
            copy.start()
        r.norm_got[pl.ds(me_x, 1)] = r.norms[...][None]
        for copy in norm_swap_x():
            copy.wait()
        total = r.norm_got[0]
        for other in range(1, groups):
            total = total + r.norm_got[other]
        r.norms[...] = total
        for copy in norm_swap_y():
            copy.start()
        r.norm_all[pl.ds(me_y, 1)] = total[None]
        for copy in norm_swap_y():
            copy.wait()
        total = r.norm_all[0]
        for other in range(1, 8):
            total = total + r.norm_all[other]
        over = 1.0 / total[15:16, 0:1]
        lanes = jnp.sum(total, axis=1, keepdims=True)
        weight_norm = jnp.sqrt(lanes[0:7])
        grad_norm = jnp.sqrt(lanes[8:15]) * over
        trust = TRUST_SCALE * weight_norm / (grad_norm + WEIGHT_DECAY * weight_norm)
        first_column = lax.broadcasted_iota(jnp.int32, (7, 2), 1) == 0
        r.norms_out[...] = jnp.where(first_column, weight_norm, grad_norm)
        for copy in gain_swap():
            copy.wait()
        gains = r.gain_got[0]
        for other in range(1, 8):
            gains = gains + r.gain_got[other]
        gains = GAIN_RATE * over * gains
        for k in range(4):
            r.new_gain_n[k] = MOMENTUM * r.gain_moment_n[k] + gains[2 * k : 2 * k + 2]
        for k in range(3):
            for which in range(2):
                for j in range(WIDE):
                    row = 8 + 8 * k + WIDE * which + j
                    here = slice(j * MID, (j + 1) * MID)
                    old = r.gain_moment_w[k, which : which + 1, here]
                    r.new_gain_w[k, which : which + 1, here] = MOMENTUM * old + gains[row : row + 1]
        for copy in flat_loads():
            copy.wait()
        outgoing = []
        for i, target in enumerate((r.new_a, r.new_b)):
            weight_ref, weight_first = weight_at[i]

            def step(index, i=i, weight_ref=weight_ref, weight_first=weight_first):
                def at(first):
                    return pl.ds(pl.multiple_of(first + index * FLAT_STEP, 32), FLAT_STEP)

                rate = jnp.zeros((FLAT_STEP, 128), F32)
                for layer in range(len(layer_bounds[i]) - 1):
                    row = layers_before[i] + layer
                    rate = jnp.where(in_layer(i, index, layer), trust[row : row + 1], rate)
                decayed = d_acc[at(share_at[i]), :] * over + WEIGHT_DECAY * weight_ref[at(weight_first), :]
                here = at(moment_at[i])
                r.flat[here, :] = MOMENTUM * r.flat[here, :] + LEARN_RATE * rate * decayed

            loop(flat_rows[i] // FLAT_STEP, step, unroll=2)
            source = r.flat.at[pl.ds(moment_at[i], flat_rows[i])]
            outgoing.append(pltpu.make_async_copy(source, target, r.hsem.at[i]))
            outgoing[-1].start()
        for copy in outgoing:
            copy.wait()

    sum_order = [(1, 3), (1, 2), (1, 1), (1, 0), (0, 3), (0, 2), (0, 1), (0, 0)]
    ticks = {}
    for u, (i, zz) in enumerate(sum_order):
        slot = u % len(work)
        before = sum_order[u - len(work)] if u >= len(work) else None
        for at_tick, rank, op in (
            (0, 5, functools.partial(sum_one_load, i, zz, slot, before)),
            (1, 2, functools.partial(sum_one, i, zz, slot)),
            (5, 4, functools.partial(sum_two_load, i, zz, slot)),
            (6, 1, functools.partial(sum_two, i, zz, slot)),
            (8, 3, functools.partial(sum_three_load, i, zz, slot)),
            (9, 0, functools.partial(sum_three, i, zz, slot)),
        ):
            ticks.setdefault(3 * u + at_tick, []).append((rank, u, op))
    pending = [
        [op for _, _, op in sorted(ticks.get(tick, []), key=lambda item: item[:2])]
        for tick in range(max(ticks) + 1)
    ]

    pending = [[]] + pending

    def pump(count=1):
        if direct:
            for _ in range(count):
                if pending:
                    for op in pending.pop(0):
                        op()

    def sums_of(*units):
        if direct:
            for i, zz in units:
                sum_send(i, zz, 0)

    def unravel(source, first, count, target, begin=0, end=None):
        end = count * WIDE // TILE if end is None else end
        part = TILE // WIDE
        depth = 2 * MID // TILE

        def raw(chunk):
            slot = lax.rem(chunk, depth)
            return pltpu.make_async_copy(
                source.at[pl.ds(pl.multiple_of(first + chunk * TILE, TILE), TILE)],
                d_out.at[columns(slot, TILE)],
                rsem.at[slot],
            )

        for chunk in range(begin, min(begin + depth - 1, end)):
            raw(jnp.int32(chunk)).start()
        lane = lax.broadcasted_iota(jnp.int32, (1, TILE), 1)
        order = one_hot(lax.rem(lane, WIDE) * part + lax.div(lane, WIDE), TILE)

        def body(step):
            chunk = step + begin

            @pl.when(chunk + depth - 1 < end)
            def _():
                raw(chunk + depth - 1).start()

            raw(chunk).wait()
            sorted_rows = dot(order, d_out[columns(lax.rem(chunk, depth), TILE), :]).astype(BF16)
            where = pl.ds(pl.multiple_of(chunk * part, part), part)
            for k in range(WIDE):
                values = sorted_rows[k * part : (k + 1) * part]
                if target.shape[1] == MID:
                    target[pl.ds(pl.multiple_of(k * count + chunk * part, part), part), :] = values
                else:
                    target[where, k * MID : (k + 1) * MID] = values

        loop(end - begin, body)

    def gather_pictures(refs, codes, step, width, target, after):
        shapes = [(side, side * step, slots) for side, slots in layout.sizes]
        turns = [(block, p) for block in range(width // MID) for p in range(step)]

        def scoped(*buffers):
            raws, flats = buffers[: len(shapes)], buffers[len(shapes) :]

            def copy_of(turn, res):
                block, p = turns[turn]
                source = refs[res].at[:, p, :, :, pl.ds(block * MID, MID)]
                return pltpu.make_async_copy(source, raws[res], isem.at[res])

            for res in range(len(shapes)):
                copy_of(0, res).start()
            for turn, (block, p) in enumerate(turns):
                for res, shape in enumerate(shapes):
                    copy_of(turn, res).wait()
                    flats[res][...] = raws[res][...].reshape(shape[0] * shape[1] * shape[2], MID)
                    if turn + 1 < len(turns):
                        copy_of(turn + 1, res).start()

                def body(index, block=block, p=p):
                    kind = 2 * p + index
                    for tile in range(tiles):
                        total = None
                        for res, shape in enumerate(shapes):
                            if tile in layout.tiles_of(res):
                                row = (tile * len(shapes) + res) * step + p
                                lanes = codes[row : row + 1, : flats[res].shape[0]]
                                term = dot(one_hot(lanes, TILE, kind * TILE), flats[res][...])
                                total = term if total is None else total + term
                        here = slice(tile * TILE, (tile + 1) * TILE)
                        target[here, columns(kind * (width // MID) + block)] = total.astype(BF16)

                loop(step, body)
                after(turn)

        pl.run_scoped(
            scoped,
            *[pltpu.VMEM((*shape, MID), BF16) for shape in shapes],
            *[pltpu.VMEM((shape[0] * shape[1] * shape[2], MID), BF16) for shape in shapes],
        )

    if direct:
        incoming = [
            pltpu.make_async_copy(source, d_acc.at[pl.ds(share_at[i], flat_rows[i])], r.hsem.at[i])
            for i, source in enumerate((wa, wb))
        ]
        for copy in incoming:
            copy.start()
        for copy in incoming:
            copy.wait()
        for i in range(2):
            for lane in range(LANE_ROWS):
                values = d_acc[pl.ds(share_at[i] + lane, counts[i], stride=LANE_ROWS), :]
                shards[i][:, lane * 128 : (lane + 1) * 128] = values.astype(BF16)
    pl.semaphore_wait(barrier, len(greeted))
    if direct:
        copies_own = [
            pltpu.make_async_copy(
                shards[i], alls[i].at[span((me_x * 8 + me_y) * counts[i], counts[i])], wsem.at[2 * i]
            )
            for i in range(2)
        ]
        for i in range(2):
            copies_own[i].start()
            for hop in range(1, groups):
                along_z(i, hop).start()
            copies_own[i].wait()
            spread_own(i, me_x)
        r.norms[...] = jnp.zeros(r.norms.shape, F32)
        for i in range(2):
            layer_squares(i, d_acc, share_at[i], 0)
    present = [counts_in[0, res] for res in range(3)]
    local_pixels = sum(
        present[res] * side * side for res, side in {(m[1], m[0]) for tile in layout.tiles for m in tile}
    ).astype(F32)
    ids = codes_row[...]
    limits = [(res << 16, (res << 16) + present[res]) for res in range(3)]
    inside = [(ids >= low) & (ids < high) for low, high in limits]
    mask[...] = jnp.where(inside[0] | inside[1] | inside[2], 1.0, 0.0)

    def copies_of(e, count):
        return [
            pltpu.make_async_remote_copy(
                src_ref=stats.at[pl.ds(FIRST[e], count)],
                dst_ref=arrived.at[me_x, pl.ds(FIRST[e], count)],
                send_sem=xsend.at[e, hop - 1],
                recv_sem=xrecv.at[e, hop - 1],
                device_id=(lax.rem(me_x + hop, groups), me_y),
                device_id_type=MESH,
            )
            for hop in range(1, groups)
        ]

    def send(e, count):
        for copy in copies_of(e, count):
            copy.start()
        here = slice(FIRST[e], FIRST[e] + count)
        arrived[pl.ds(me_x, 1), here] = stats[here][None]

    def receive(e, count):
        for copy in copies_of(e, count):
            copy.wait()
        here = slice(FIRST[e], FIRST[e] + count)
        total = arrived[0, here]
        for other in range(1, groups):
            total = total + arrived[other, here]
        totals[e, :count] = total

    def each(width, body):
        def step(index):
            block, step_row = index // steps, lax.rem(index, steps)
            body(pl.ds(pl.multiple_of(step_row * ROWS, ROWS), ROWS), block)

        loop(width * steps, step, unroll=4)

    def each_sums(width, body, e, targets):
        def block_step(block):
            def step(index, carry):
                values = body(pl.ds(pl.multiple_of(index * ROWS, ROWS), ROWS), block)
                return tuple(
                    kept + jnp.sum(value.reshape(ROWS // 8, 8, MID), axis=0)
                    for kept, value in zip(carry, values)
                )

            start = tuple(jnp.zeros((8, MID), F32) for _ in targets(0))
            sums = lax.fori_loop(0, steps, step, start, unroll=4)
            for row, value in zip(targets(block), sums):
                stats[pl.ds(FIRST[e] + row, 1)] += jnp.sum(value, axis=0, keepdims=True)

        loop(width, block_step)

    def moments(source, e, width, same=False, first=0):
        def body(here, block):
            value = source[here, columns(block)].astype(F32)
            kept = value * mask[here, :]
            return kept, kept * value

        if same:
            each_sums(width, body, e, lambda block: (first, first + 1))
        else:
            each_sums(width, body, e, lambda block: (first + block, first + width + block))

    def pixel_row():
        return totals[0, 2:3]

    def coefficients(e, first, width, gain_rows, k, pixel_scale):
        count = pixel_row() * pixel_scale
        for j in range(width):
            center = totals[e, first + j : first + j + 1] / count
            square = totals[e, first + width + j : first + width + j + 1] / count
            factor = lax.rsqrt(square - center * center + EPSILON)
            gain, offset = gain_rows(j)
            scale = gain * factor
            par[k, j : j + 1] = scale
            par[k, width + j : width + j + 1] = offset - center * scale
            par[k, 2 * width + j : 2 * width + j + 1] = factor
            par[k, 3 * width + j : 3 * width + j + 1] = -center * factor

    def narrow_gains(k):
        return lambda j: (gains_n[k, 0:1, :], gains_n[k, 1:2, :])

    def wide_gains(k):
        return lambda j: (
            gains_w[k, 0:1, j * MID : (j + 1) * MID],
            gains_w[k, 1:2, j * MID : (j + 1) * MID],
        )

    def row_of(k, which, width, block):
        return par[k, pl.ds(which * width + block, 1)]

    def back_coefficients(e, sum_first, cross_first, width, k, pixel_scale):
        count = pixel_row() * pixel_scale
        for j in range(width):
            total_g = totals[e, sum_first + j : sum_first + j + 1]
            total_x = totals[e, cross_first + j : cross_first + j + 1]
            scale = par[k, j : j + 1]
            factor = par[k, 2 * width + j : 2 * width + j + 1]
            shift = par[k, 3 * width + j : 3 * width + j + 1]
            par[k + 8, j : j + 1] = scale * (total_g + shift * total_x) / count
            par[k + 8, width + j : width + j + 1] = scale * factor * total_x / count

    def activate(source, target, k):
        def body(here, block):
            value = source[here, columns(block)].astype(F32)
            value = value * row_of(k, 0, 1, 0) + row_of(k, 1, 1, 0)
            target[here, columns(block)] = (value * sigmoid(value)).astype(BF16)

        each(source.shape[1] // MID, body)

    def slope(value):
        s = sigmoid(value)
        return s * (1.0 + value * (1.0 - s))

    def back_activate(grad, source, k, e, same=False):
        def body(here, block):
            z = source[here, columns(block)].astype(F32)
            g = grad[here, columns(block)] * slope(z * row_of(k, 0, 1, 0) + row_of(k, 1, 1, 0))
            grad[here, columns(block)] = g
            return g, g * (z * row_of(k, 2, 1, 0) + row_of(k, 3, 1, 0))

        each_sums(source.shape[1] // MID, body, e, lambda block: (0, 1))

    def back_norm(grad, source, target, k, width, same=False):
        def body(here, block):
            j = 0 if same else block
            z = source(here, block) if callable(source) else source[here, columns(block)].astype(F32)
            g = grad[here, columns(block)]
            fixed = row_of(k + 8, 0, width, j) + z * row_of(k + 8, 1, width, j)
            value = g * row_of(k, 0, width, j) - mask[here, :] * fixed
            target[here, columns(block)] = value.astype(BF16)

        each(target.shape[1] // MID, body)

    def shift_into(source, block, table_row, target):
        for tile in range(tiles):
            here = slice(tile * TILE, (tile + 1) * TILE)
            pick = one_hot(shifts[pl.ds(table_row, 1), here], TILE)
            target[here, :] = dot(pick, source[here, columns(block)]).astype(BF16)

    def strided_tap(tap):
        p, q = tap // 3, lax.rem(tap, 3)
        kind = 2 * lax.rem(p + 1, 2) + lax.rem(q + 1, 2)
        return kind, ((p + 1) // 2) * 3 + (q + 1) // 2

    def tap_weight(tap):
        return w_sp[columns(tap), :]

    stats[...] = jnp.zeros(stats.shape, F32)

    image_places = {1: 0, 3: 1}
    gather_pictures(
        (img_s, img_m, img_l),
        codes_img,
        2,
        C_IN,
        x_p,
        lambda turn: pass_on(image_places[turn]) if turn in image_places else None,
    )
    cot_places = {1: 2, 3: 3}
    gather_pictures(
        (cot_s, cot_m, cot_l),
        codes_cot,
        1,
        C_OUT,
        cot_p,
        lambda turn: pass_on(cot_places[turn]) if turn in cot_places else None,
    )
    done(0, 0)
    get_ra.start()
    get_sa_low.start()
    get_ra.wait()

    def first_product(kind):
        z_one[:, columns(kind)] = dot(x_p[:, columns(kind, C_IN)], w_ra[...]).astype(z_one.dtype)

    loop(4, first_product)
    moments(z_one, 0, 4, same=True)
    stats[2:3] = jnp.full((1, MID), local_pixels, F32)
    send(0, 8)
    pass_on(4)
    done(0, 1)
    get_sa_high.start()
    receive(0, 8)
    coefficients(0, 0, 1, narrow_gains(0), 0, 4.0)
    activate(z_one, act_one, 0)

    pass_on(5)
    get_sa_low.wait()
    get_sa_high.wait()
    z_two[...] = jnp.zeros(z_two.shape, F32)

    def conv_a(tap):
        kind, table_row = strided_tap(tap)
        shift_into(act_one, kind, 8 - table_row, shifted)
        z_two[...] += dot(shifted[...], tap_weight(tap))

    for start in range(0, 9, 3):
        loop(3, lambda step, start=start: conv_a(start + step), 3)
        pass_on(6 + start // 3)
    moments(z_two, 1, 1)
    send(1, 8)
    pass_on(9)
    done(0, 2)
    unravel(full_a, ROW_EA, MID, w_ea)
    ready = max(8 * 3 * counts[0] - ROW_PA, 0) // TILE if direct else 0
    if ready:
        unravel(full_a, ROW_PA, C_IN, w_pa, 0, ready)
    pass_on(10)
    done(0, 3)
    unravel(full_a, ROW_PA, C_IN, w_pa, ready)

    def side_product(block):
        z_side[:, columns(block)] = dot(x_p[:, :C_IN], w_pa[:, columns(block)]).astype(z_side.dtype)

    loop(WIDE, side_product)
    pass_on(11)
    moments(z_side, 2, WIDE, first=8)
    receive(1, 8)
    coefficients(1, 0, 1, narrow_gains(1), 1, 1.0)
    activate(z_two, act_two, 1)

    def main_product(block):
        z_main[:, columns(block)] = dot(act_two[...], w_ea[:, columns(block)]).astype(z_main.dtype)

    loop(WIDE, main_product)
    moments(z_main, 2, WIDE)
    pass_on(12)
    send(2, 16)
    pass_on(13)
    done(1, 0)
    get_rb.start()
    receive(2, 16)
    coefficients(2, 0, WIDE, wide_gains(0), 4, 1.0)
    coefficients(2, 8, WIDE, wide_gains(1), 5, 1.0)

    def joined_a(here, block):
        main = z_main[here, columns(block)].astype(F32)
        side = z_side[here, columns(block)].astype(F32)
        value = main * row_of(4, 0, WIDE, block) + row_of(4, 1, WIDE, block)
        return main, side, value + side * row_of(5, 0, WIDE, block) + row_of(5, 1, WIDE, block)

    def block_rows(here, block):
        return pl.ds(pl.multiple_of(block * rows + here.start, ROWS), ROWS)

    def middle_step(here, block):
        _, _, value = joined_a(here, block)
        middle[block_rows(here, block), :] = (value * sigmoid(value)).astype(BF16)

    each(WIDE, middle_step)
    pass_on(14)
    get_rb.wait()
    four = dot(middle[columns(0), :], w_rb[columns(0), :])
    for block in range(1, WIDE):
        four = four + dot(middle[columns(block), :], w_rb[columns(block), :])
    z_four[...] = four
    moments(z_four, 3, 1)
    send(3, 8)
    for zz in range(1, 4):
        done(1, zz)
    get_sb.start()
    unravel(full_b, ROW_EB, MID, w_eb)
    receive(3, 8)
    coefficients(3, 0, 1, narrow_gains(2), 2, 1.0)
    activate(z_four, act_four, 2)

    get_sb.wait()
    z_five[...] = jnp.zeros(z_five.shape, F32)

    def conv_b(tap):
        shift_into(act_four, 0, 8 - tap, shifted)
        z_five[...] += dot(shifted[...], tap_weight(tap))

    loop(9, conv_b, 3)
    moments(z_five, 4, 1)
    send(4, 8)
    receive(4, 8)
    coefficients(4, 0, 1, narrow_gains(3), 3, 1.0)
    activate(z_five, act_five, 3)

    def last_product(block):
        z_six[columns(block), :] = dot(act_five[...], w_eb[columns(block), :]).astype(z_six.dtype)

    loop(WIDE, last_product)
    def six(here, block):
        return z_six[block_rows(here, block), :].astype(F32)

    def last_moments(here, block):
        value = six(here, block)
        kept = value * mask[here, :]
        return kept, kept * value

    each_sums(WIDE, last_moments, 5, lambda block: (block, WIDE + block))
    send(5, 8)
    receive(5, 8)
    coefficients(5, 0, WIDE, wide_gains(2), 6, 1.0)

    if direct:
        for i in range(2):
            for hop in range(1, groups):
                along_z(i, hop).wait_send()

    def turn_over(array, row=0, block=0):
        here = (pl.ds(row, MID), columns(block))
        array[here] = array[here].T

    def output_step(here, block):
        z = six(here, block)
        value = z * row_of(6, 0, WIDE, block) + row_of(6, 1, WIDE, block)
        value = value + middle[block_rows(here, block), :].astype(F32)
        g = cot_p[here, columns(block)].astype(F32) * mask[here, :] * slope(value)
        g_wide[here, columns(block)] = g
        return g, g * (z * row_of(6, 2, WIDE, block) + row_of(6, 3, WIDE, block))

    each_sums(WIDE, output_step, 6, lambda block: (block, WIDE + block))
    send(6, 8)
    turn_over(act_five)
    turn_over(act_four)
    turn_over(act_two)
    receive(6, 8)
    back_coefficients(6, 0, WIDE, WIDE, 6, 1.0)
    gp_six = cot_p
    back_norm(g_wide, six, gp_six, 6, WIDE)

    def put(unit, first, target, slot):
        return pltpu.make_async_copy(
            d_out.at[columns(slot)],
            target.at[pl.ds(pl.multiple_of(first + unit * MID, MID), MID)],
            dsem.at[slot],
        )

    def store_unit(step, first, target, value, unit=None):
        slot = lax.rem(step, 2) if not isinstance(step, int) else step % 2
        unit = step if unit is None else unit

        @pl.when(step >= 2)
        def _():
            put(unit, first, target, slot).wait()

        d_out[columns(slot), :] = value.astype(BF16)
        put(unit, first, target, slot).start()

    def flush_one(slot, first, target):
        put(0, first, target, slot).wait()

    def flush(first, target):
        for slot in range(2):
            flush_one(slot, first, target)

    def wide_weight_grad(left, left_count, grad, first, target):
        def body(chunk):
            part = left(chunk)
            for k in range(WIDE):
                value = dot(part, grad[:, columns(k)])
                for lane in range(LANE_ROWS):
                    where = pl.ds(lane * WIDE * TILE + k, TILE, stride=WIDE)
                    d_acc[where, :] = value[:, lane * 128 : (lane + 1) * 128]
            for half in range(2):
                firsts = [lane * WIDE * TILE + half * MID for lane in range(LANE_ROWS)]
                value = jnp.concatenate([d_acc[first : first + MID, :] for first in firsts], axis=1)
                store_unit(chunk * 2 + half, first, target, value)

        loop(left_count // TILE, body)
        flush(first, target)

    g_five = dot_nt(gp_six[:, columns(0)], w_eb[columns(0), :])
    for block in range(1, WIDE):
        g_five = g_five + dot_nt(gp_six[:, columns(block)], w_eb[columns(block), :])
    g_nar[...] = g_five
    back_activate(g_nar, z_five, 3, 7)
    send(7, 8)
    wide_weight_grad(lambda chunk: act_five[columns(chunk, TILE), :], MID, gp_six, ROW_EB, dwb)
    receive(7, 8)
    back_coefficients(7, 0, 1, 1, 3, 1.0)
    back_norm(g_nar, z_five, gp_nar, 3, 1)

    g_nar[...] = jnp.zeros(g_nar.shape, F32)

    def conv_b_back(step, tap):
        shift_into(gp_nar, 0, tap, shifted)
        g_nar[...] += dot_nt(shifted[...], tap_weight(tap))
        store_unit(step, ROW_SB, dwb, dot(act_four[...], shifted[...]), tap)

    low_two = (2 * 8 * counts[1] - ROW_SB) // MID if direct else 0
    conv_b_back(0, 8)
    flush_one(0, ROW_SB, dwb)
    sums_of((1, 3))
    loop(8 - low_two, lambda step: conv_b_back(step, 7 - step), 2)
    flush(ROW_SB, dwb)
    sums_of((1, 2))
    pump()
    loop(low_two, lambda step: conv_b_back(step, low_two - 1 - step), 2)
    get_sa.start()
    flush(ROW_SB, dwb)
    sums_of((1, 1))
    pump()
    back_activate(g_nar, z_four, 2, 8)
    send(8, 8)
    pump()
    receive(8, 8)
    back_coefficients(8, 0, 1, 1, 2, 1.0)
    back_norm(g_nar, z_four, gp_nar, 2, 1)
    pump()

    def middle_back(block):
        g_wide[:, columns(block)] += dot_nt(gp_nar[...], w_rb[columns(block), :])

    loop(WIDE, middle_back)
    pump()

    def join_step(here, block):
        main, side, value = joined_a(here, block)
        g = g_wide[here, columns(block)] * slope(value)
        g_wide[here, columns(block)] = g
        return (
            g,
            g * (main * row_of(4, 2, WIDE, block) + row_of(4, 3, WIDE, block)),
            g * (side * row_of(5, 2, WIDE, block) + row_of(5, 3, WIDE, block)),
        )

    each_sums(WIDE, join_step, 9, lambda block: (block, WIDE + block, 2 * WIDE + block))
    send(9, 16)
    pump()
    for kind in range(4):
        turn_over(act_one, 0, kind)

    def reduce_b_grad(block):
        store_unit(block, ROW_RB, dwb, dot_tn(middle[columns(block), :], gp_nar[...]))

    loop(WIDE, reduce_b_grad)
    flush(ROW_RB, dwb)
    sums_of((1, 0))
    pump()
    receive(9, 16)
    back_coefficients(9, 0, WIDE, WIDE, 4, 1.0)
    back_coefficients(9, 0, 2 * WIDE, WIDE, 5, 1.0)
    gp_main = cot_p
    back_norm(g_wide, z_main, gp_main, 4, WIDE)
    pump()
    g_nar[...] = dot_nt(gp_main[...], w_ea[...])
    back_activate(g_nar, z_two, 1, 10)
    send(10, 8)
    back_norm(g_wide, z_side, gp_side, 5, WIDE)
    pump()
    wide_weight_grad(lambda chunk: x_p[:, columns(chunk, TILE)].T, C_IN, gp_side, ROW_PA, dwa)
    sums_of((0, 3))
    pump()
    wide_weight_grad(lambda chunk: act_two[columns(chunk, TILE), :], MID, gp_main, ROW_EA, dwa)
    sums_of((0, 2))
    pump()
    receive(10, 8)
    back_coefficients(10, 0, 1, 1, 1, 1.0)
    back_norm(g_nar, z_two, gp_nar, 1, 1)
    pump()

    get_sa.wait()
    g_one = g_wide
    g_one[...] = jnp.zeros(g_one.shape, F32)

    def conv_a_back(tap):
        kind, table_row = strided_tap(tap)
        shift_into(gp_nar, 0, table_row, shifted)
        g_one[:, columns(kind)] += dot_nt(shifted[...], tap_weight(tap))

    for start in range(0, 9, 3):
        loop(3, lambda step, start=start: conv_a_back(start + step), 3)
        pump()
    back_activate(g_one, z_one, 0, 11)
    send(11, 8)
    pump()

    def conv_a_grad(step, tap):
        kind, table_row = strided_tap(tap)
        shift_into(gp_nar, 0, table_row, shifted)
        store_unit(step, ROW_SA, dwa, dot(act_one[:, columns(kind)], shifted[...]), tap)

    low_one = (8 * counts[0] - ROW_SA) // MID if direct else 0
    loop(9 - low_one, lambda step: conv_a_grad(step, 8 - step), 3)
    flush(ROW_SA, dwa)
    sums_of((0, 1))
    pump()
    if low_one:
        loop(low_one, lambda step: conv_a_grad(step, low_one - 1 - step), 3)
        flush(ROW_SA, dwa)
    pump()
    receive(11, 8)
    if direct:
        start_gains()
        for copy in flat_loads()[1:]:
            copy.start()
    back_coefficients(11, 0, 1, 1, 0, 4.0)
    gp_one = act_one
    back_norm(g_one, z_one, gp_one, 0, 1, same=True)

    for half in range(C_IN // MID):
        total = None
        for kind in range(4):
            left = x_p[:, kind * C_IN + half * MID : kind * C_IN + (half + 1) * MID]
            term = dot_tn(left, gp_one[:, columns(kind)])
            total = term if total is None else total + term
        store_unit(half, ROW_RA, dwa, total)
    flush(ROW_RA, dwa)
    sums_of((0, 0))
    pump()

    def image_back(kind):
        value = dot_nt(gp_one[:, columns(kind)], w_ra[...])
        x_p[:, columns(kind, C_IN)] = value.astype(BF16)

    x_side = dot_nt(gp_one[:, :MID], w_ra[...]) + dot_nt(gp_side[...], w_pa[...])
    x_p[:, :C_IN] = x_side.astype(BF16)
    for kind in range(1, 4):
        image_back(kind)
        pump()

    outs = (out_s, out_m, out_l)
    for res, (side, slots) in enumerate(layout.sizes):
        used = layout.tiles_of(res)
        here = slice(used[0] * TILE, (used[-1] + 1) * TILE)
        count = side * 2 * side * slots

        def scoped(raw, res=res, side=side, slots=slots, here=here, count=count):
            def copy_of(p):
                return pltpu.make_async_copy(raw.at[p], outs[res].at[:, p], isem.at[p])

            for p in range(2):
                row = 2 * res + p
                for block in range(C_IN // MID):
                    total = None
                    for q in range(2):
                        lanes = codes_back[row : row + 1, q * rows + here.start : q * rows + here.stop]
                        first = (2 * p + q) * C_IN + block * MID
                        term = dot(one_hot(lanes, count), x_p[here, first : first + MID])
                        total = term if total is None else total + term
                    total = total.astype(BF16).reshape(side, 2 * side, slots, MID)
                    raw[p, :, :, :, block * MID : (block + 1) * MID] = total
                copy_of(p).start()
                pump()
            for p in range(2):
                copy_of(p).wait()

        pl.run_scoped(scoped, pltpu.VMEM((2, side, 2 * side, slots, C_IN), BF16))

    if not direct:
        return
    pump(len(pending))
    for i in range(2):
        last_sum(i, share_at[i])
    flat_loads()[0].start()
    for i in range(2):
        layer_squares(i, d_acc, share_at[i], 8)
    r.norms[15:16, :] = jnp.full((1, 128), local_pixels, F32)
    update()

    for i in range(2):
        for zz in range(groups):
            for k in range(len(spread_plan)):
                spread(i, zz, k).wait_send()
            for k in range(4):
                piece(i, zz, 0, k).wait_send()

            @pl.when(zz != me_x)
            def _(i=i, zz=zz):
                to_z(i, zz).wait_send()

    for u in range(len(sum_order) - len(work), len(sum_order)):
        for k in range(4, 10):
            piece(*sum_order[u], u % len(work), k).wait_send()


def both_blocks(groups, direct, images, cots, wa, wb, gains, counts, moments):
    layout = Layout([image.shape for image in images])
    rows = layout.rows
    img_codes = layout.picture_rows(2)
    cot_codes = layout.picture_rows(1)

    def by_pixel(picture, step):
        turned = jnp.transpose(picture, (1, 2, 0, 3))
        return turned.reshape(turned.shape[0] // step, step, *turned.shape[1:])

    def table(codes):
        width = round_up(max(code.shape[0] for code in codes), 128)
        result = np.full((round_up(len(codes), 8), width), -1, np.int32)
        for index, code in enumerate(codes):
            result[index, : code.shape[0]] = code
        return jnp.asarray(result)

    back = layout.picture_back()
    back = np.concatenate([back, np.full((round_up(len(back), 8) - len(back), back.shape[1]), -1, np.int32)])
    anywhere = pl.BlockSpec(memory_space=pl.ANY)
    vmem = pl.BlockSpec(memory_space=pltpu.VMEM)
    wide16 = pltpu.VMEM((rows, C_OUT), BF16)
    wide32 = pltpu.VMEM((rows, C_OUT), F32)
    nar16 = pltpu.VMEM((rows, MID), BF16)
    nar32 = pltpu.VMEM((rows, MID), F32)
    shapes = [
        *[jax.ShapeDtypeStruct(by_pixel(image, 2).shape, BF16) for image in images],
        jax.ShapeDtypeStruct((END_A, MID), BF16),
        jax.ShapeDtypeStruct((END_B, MID), BF16),
        jax.ShapeDtypeStruct((EXCHANGES, 16, MID), F32),
    ]
    scratch = [
        *[wide16, wide16, wide16, pltpu.VMEM((WIDE * rows, MID), BF16), wide32],
        pltpu.VMEM((WIDE * rows, MID), BF16),
        *[wide16] * 3,
        *[nar32] * 4,
        *[nar16] * 5,
        pltpu.VMEM((rows, 4 * C_IN), BF16),
        pltpu.VMEM((C_IN, MID), BF16),
        pltpu.VMEM((9 * MID, MID), BF16),
        pltpu.VMEM((MID, C_OUT), BF16),
        pltpu.VMEM((C_IN, C_OUT), BF16),
        pltpu.VMEM((C_OUT, MID), BF16),
        pltpu.VMEM((C_OUT, MID), BF16),
        pltpu.VMEM((LANE_ROWS * WIDE * TILE, 128), F32),
        pltpu.VMEM((2 * MID, MID), BF16),
        pltpu.VMEM((SUM_ROWS, MID), F32),
        pltpu.VMEM((groups, SUM_ROWS, MID), F32),
        pltpu.VMEM((16, 16, MID), F32),
        pltpu.VMEM((rows, 1), F32),
        pltpu.SemaphoreType.DMA((5,)),
        pltpu.SemaphoreType.DMA((2 * MID // TILE,)),
        pltpu.SemaphoreType.DMA((2,)),
        pltpu.SemaphoreType.DMA((len(images),)),
        pltpu.SemaphoreType.DMA((EXCHANGES, groups - 1)),
        pltpu.SemaphoreType.DMA((EXCHANGES, groups - 1)),
    ]
    names = INPUTS + (DIRECT_INPUTS if direct else []) + OUTPUTS
    places = [anywhere] * 5 + [vmem]
    if direct:
        count_a, count_b = wa.shape[0] // LANE_ROWS, wb.shape[0] // LANE_ROWS
        names = names + DIRECT_OUTPUTS
        shapes += [jax.ShapeDtypeStruct(value.shape, F32) for value in (wa, wb, *gains)]
        shapes += [jax.ShapeDtypeStruct((7, 2), F32)]
        shapes += [jax.ShapeDtypeStruct((count, MID), BF16) for count in (END_A, END_B)]
        for per in (4, 2, 1, 1):
            shapes += [jax.ShapeDtypeStruct((groups * per * n, MID), BF16) for n in (count_a, count_b)]
        places += [anywhere] * 2 + [vmem] * 3 + [anywhere] * (len(DIRECT_OUTPUTS) - 5)
        scratch += [
            pltpu.VMEM((4 * count_a, MID), BF16),
            pltpu.VMEM((2 * count_a, MID), BF16),
            pltpu.VMEM((count_a, MID), BF16),
            pltpu.VMEM((groups * count_b, MID), BF16),
            pltpu.VMEM((LANE_ROWS * (count_a + 2 * count_b), 128), F32),
            pltpu.VMEM((32, MID), F32),
            pltpu.VMEM((8, 32, MID), F32),
            pltpu.VMEM((16, 128), F32),
            pltpu.VMEM((groups, 16, 128), F32),
            pltpu.VMEM((8, 16, 128), F32),
            pltpu.SemaphoreType.DMA((8,)),
            pltpu.SemaphoreType.DMA((2 * groups, 9)),
            pltpu.SemaphoreType.DMA((2 * groups, 9)),
            pltpu.SemaphoreType.DMA((2, groups - 1)),
            pltpu.SemaphoreType.DMA((2, groups)),
            pltpu.SemaphoreType.DMA((2 * groups, 11)),
            pltpu.SemaphoreType.DMA((2 * groups, 11)),
            pltpu.SemaphoreType.DMA((4,)),
            pltpu.SemaphoreType.DMA((7,)),
            pltpu.SemaphoreType.DMA((7,)),
            pltpu.SemaphoreType.DMA((groups - 1,)),
            pltpu.SemaphoreType.DMA((groups - 1,)),
            pltpu.SemaphoreType.DMA((7,)),
            pltpu.SemaphoreType.DMA((7,)),
        ]
    names = names + SCRATCH + (DIRECT_SCRATCH if direct else [])
    out = pl.pallas_call(
        functools.partial(mega, names, layout, groups, direct),
        out_shape=shapes,
        in_specs=[anywhere] * 8
        + [vmem] * 7
        + [pl.BlockSpec(memory_space=pltpu.SMEM)]
        + ([anywhere] * 2 + [vmem] * 2 if direct else []),
        out_specs=places,
        scratch_shapes=scratch,
        compiler_params=pltpu.CompilerParams(
            collective_id=0, has_side_effects=True, vmem_limit_bytes=125 * 512 * 1024
        ),
    )(
        *[by_pixel(image, 2) for image in images],
        *[by_pixel(cot, 1) for cot in cots],
        wa,
        wb,
        *gains,
        jnp.asarray(layout.neighbours()),
        table(img_codes),
        table(cot_codes),
        jnp.asarray(back),
        jnp.asarray(layout.row_codes()),
        counts,
        *(moments if direct else ()),
    )
    image_grads = [
        jnp.transpose(grad.reshape(-1, *grad.shape[2:]), (2, 0, 1, 3)) for grad in out[: len(images)]
    ]
    return (*image_grads, *out[len(images) :])


def layer_masks(first, count, bounds):
    position = first + jnp.arange(count, dtype=jnp.int32)
    rows = [(position >= low) & (position < high) for low, high in zip(bounds[:-1], bounds[1:])]
    return jnp.stack(rows).astype(F32)


def body(
    image_small,
    image_medium,
    image_large,
    cot_small,
    cot_medium,
    cot_large,
    counts,
    weights_a,
    weights_b,
    moment_a,
    moment_b,
    gains_narrow,
    gains_wide,
    gain_moment_narrow,
    gain_moment_wide,
):
    images = (image_small, image_medium, image_large)
    cots = (cot_small, cot_medium, cot_large)
    groups = lax.axis_size("gx")
    rows_a = weights_a.shape[0] // MID
    rows_b = weights_b.shape[0] // MID
    gains = (gains_narrow, gains_wide)
    direct = groups == 4 and lax.axis_size("gy") == 8 and rows_a % 16 == 0 and rows_b % 16 == 0
    if direct:
        flats = [value.reshape(-1, 128) for value in (weights_a, weights_b, moment_a, moment_b)]
        moments = (*flats[2:], gain_moment_narrow, gain_moment_wide)
        out = both_blocks(groups, direct, images, cots, *flats[:2], gains, counts, moments)
        return (*out[:3], out[6].reshape(-1), out[7].reshape(-1), *out[8:11])
    sides = [image.shape[1] // 2 for image in images]
    local_pixels = sum(counts[0, r] * sides[r] ** 2 for r in range(3)).astype(F32)
    flat_a = weights_a.reshape(rows_a, MID)
    flat_b = weights_b.reshape(rows_b, MID)
    wa = lax.all_gather(flat_a.astype(BF16), ("gx", "gy"), axis=0, tiled=True)
    wb = lax.all_gather(flat_b.astype(BF16), ("gx", "gy"), axis=0, tiled=True)
    out = both_blocks(groups, direct, images, cots, wa, wb, gains, counts, ())
    image_grads, (dwa, dwb, totals) = out[:3], out[3:6]

    def scattered(grads):
        return lax.psum_scatter(grads, ("gx", "gy"), scatter_dimension=0, tiled=True).astype(F32)

    share_a, share_b = scattered(dwa), scattered(dwb)
    device = lax.axis_index(("gx", "gy"))
    masks_a = layer_masks(device * rows_a, rows_a, [ROW_RA, ROW_SA, ROW_EA, ROW_PA, END_A])
    masks_b = layer_masks(device * rows_b, rows_b, [ROW_RB, ROW_SB, ROW_EB, END_B])

    def layer_squares(masks, flat):
        return jnp.sum(masks * jnp.sum(flat * flat, axis=1)[None, :], axis=1)

    weight_squares = jnp.concatenate([layer_squares(masks_a, flat_a), layer_squares(masks_b, flat_b)])
    grad_squares = jnp.concatenate([layer_squares(masks_a, share_a), layer_squares(masks_b, share_b)])
    partial_norms = jnp.stack([weight_squares, grad_squares], axis=1)

    def narrow(e):
        return jnp.stack([totals[e, 1], totals[e, 0]])

    def wide(e, cross):
        return jnp.stack(
            [totals[e, cross : cross + WIDE].reshape(-1), totals[e, :WIDE].reshape(-1)]
        )

    sums_narrow = jnp.stack([narrow(11), narrow(10), narrow(8), narrow(7)])
    sums_wide = jnp.stack([wide(9, WIDE), wide(9, 2 * WIDE), wide(6, WIDE)])
    total_narrow, total_wide = lax.psum((sums_narrow, sums_wide), "gy")
    total_norms, pixels_total = lax.psum((partial_norms, local_pixels), ("gx", "gy"))
    weight_norm = jnp.sqrt(total_norms[:, 0])
    grad_norm = jnp.sqrt(total_norms[:, 1]) / pixels_total
    trust_ratio = TRUST_SCALE * weight_norm / (grad_norm + WEIGHT_DECAY * weight_norm)

    def update(masks, trust, share, flat, moment):
        trust_rows = jnp.sum(masks * trust[:, None], axis=0)[:, None]
        step = LEARN_RATE * trust_rows * (share / pixels_total + WEIGHT_DECAY * flat)
        return MOMENTUM * moment + step.reshape(-1)

    return (
        *image_grads,
        update(masks_a, trust_ratio[:4], share_a, flat_a, moment_a),
        update(masks_b, trust_ratio[4:], share_b, flat_b, moment_b),
        MOMENTUM * gain_moment_narrow + GAIN_RATE * (total_narrow / pixels_total),
        MOMENTUM * gain_moment_wide + GAIN_RATE * (total_wide / pixels_total),
        jnp.stack([weight_norm, grad_norm], axis=1),
    )


def solution(mesh):
    split = P(("gx", "gy"))
    in_specs = (split,) * 11 + (P(),) * 4
    out_specs = (split,) * 5 + (P(),) * 3
    return jax.shard_map(body, mesh=mesh, in_specs=in_specs, out_specs=out_specs, check_vma=False)
```
